128 devices in a mesh: seq: 16 (over y, z), tp: 8 (over x, core).
Axes of the slice: x: 4, y: 4, z: 4, core: 2. Of those that a mesh axis runs over, the one named last changes fastest.
Arguments:
- queries: bfloat16 [2048, 8192], P('seq', 'tp'), may hold values from -8 to 8
- prompt_prefix_keys: bfloat16 [32768, 1024], P('seq', 'tp'), may hold values from -8 to 8
- prompt_prefix_values: bfloat16 [32768, 1024], P('seq', 'tp'), may hold values from -6 to 6
- continuation_keys: bfloat16 [2048, 1024], P('seq', 'tp'), may hold values from -8 to 8
- continuation_values: bfloat16 [2048, 1024], P('seq', 'tp'), may hold values from -6 to 6
- owners: int32 [64, 4], P('seq'), may hold values from 0 to 15, all different within a row; in each aligned block of 4 rows (0 to 3, 4 to 7, ...) at most 2 rows name the same one
- lengths: int32 [64], P('seq'), may hold values from 1 to 32, 1280 in all
- out_weight: bfloat16 [8192, 8192], P('tp'), may hold values from -2.5 to 2.5
Outputs:
- mixed: bfloat16 [2048, 8192], P(('seq', 'tp'))
The draws below stay inside these ranges and needn't reach their ends.
Inputs may be any that keep to these rules, and one draw needn't show every extreme that they name: Each row names 4 different owners. Among the 4 branches of one index of seq no owner is named more than 2 times, and in every draw some owner is named exactly 2 times by the branches of some index. `lengths`: the largest length equals 32.
All inputs are finite; a program needn't handle non-finite values. No bound on the sum of `lengths` on one device may be relied on, other than what follows from the above.
Results may differ from the reference program's by a relative error of at most 0.0055.
Values may be sent and summed in bfloat16 or wider, within the bound.
A program may use at most 128 MiB of HBM per device.

```python
import math
import jax
import jax.numpy as jnp
import numpy as np
from jax import lax

D = 8192
QUERY_HEADS = 64
KEY_VALUE_HEADS = 8
HEAD_WIDTH = 128
SUFFIX_SLOTS = 32
PREFIX_PER_OWNER = 2048
BR_DEV = 4
FAN = 4
CAP = 2
BRANCH_TOTAL = 64
TOKEN_SLOTS = 2048
PREFIX_TOKENS = 32768
N_SEQ = 16


def context_part(key):
    return 0.6 * jnp.clip(jax.random.normal(key, (BRANCH_TOTAL, KEY_VALUE_HEADS * HEAD_WIDTH), jnp.float32), -3.3, 3.3)


def draw_queries(key, part):
    context_vectors = context_part(key)
    key = jax.random.fold_in(key, 3)
    group_size = QUERY_HEADS // KEY_VALUE_HEADS
    noise_values = jnp.clip(jax.random.normal(key, (BRANCH_TOTAL, SUFFIX_SLOTS, KEY_VALUE_HEADS, group_size, HEAD_WIDTH), jnp.float32), -6.0, 6.0)
    value_rows = noise_values + context_vectors.reshape(BRANCH_TOTAL, 1, KEY_VALUE_HEADS, 1, HEAD_WIDTH)
    return value_rows.reshape(TOKEN_SLOTS, QUERY_HEADS * HEAD_WIDTH).astype(jnp.bfloat16)


def draw_prompt_prefix_keys(key, part):
    key = jax.random.fold_in(key, 5)
    value_rows = jnp.clip(jax.random.normal(key, (PREFIX_TOKENS, KEY_VALUE_HEADS * HEAD_WIDTH), jnp.float32), -6.0, 6.0)
    return value_rows.astype(jnp.bfloat16)


def draw_continuation_keys(key, part):
    context_vectors = context_part(key)
    key = jax.random.fold_in(key, 7)
    noise_values = jnp.clip(jax.random.normal(key, (BRANCH_TOTAL, SUFFIX_SLOTS, KEY_VALUE_HEADS * HEAD_WIDTH), jnp.float32), -6.0, 6.0)
    value_rows = noise_values + context_vectors[:, None, :]
    return value_rows.reshape(TOKEN_SLOTS, KEY_VALUE_HEADS * HEAD_WIDTH).astype(jnp.bfloat16)


def block_scale(own_key, shape, shards, smallest, top_value):
    factor_of = 1.0
    for position, parts in shards:
        draws = jax.random.uniform(jax.random.fold_in(jax.random.fold_in(own_key, 6), position), (parts,), jnp.float32, smallest / len(shards), top_value / len(shards))
        factor_of = factor_of * jnp.repeat(jnp.exp(draws), shape[position] // parts).reshape((-1,) + (1,) * (len(shape) - 1 - position))
    return factor_of


def profile(amount, total, reach, slope):
    weights = [(1 << 20) // math.isqrt(grade ** slope) + 1 for grade in range(2, amount + 1)]
    spare, given = total - reach - (amount - 1), [1] * (amount - 1)
    while spare > 0:
        candidates = [i for i in range(amount - 1) if given[i] < reach]
        whole, budget = sum([weights[i] for i in candidates]), spare
        for i in candidates:
            more = min(reach - given[i], max(1, budget * weights[i] // whole), spare)
            given[i] = given[i] + more
            spare = spare - more
    return np.array([reach] + given)


def ragged(stream_key, number_of, total, most, slope):
    if number_of == 2:
        one = jax.random.randint(stream_key, (), max(1, total - most), min(most, total - 1) + 1)
        return jnp.stack([one, total - one])
    tallies = jnp.asarray(profile(number_of, total, most, slope), jnp.int32)
    couples = (number_of - 1) // 2
    giver, taker = tallies[1:1 + 2 * couples:2], tallies[2:2 + 2 * couples:2]
    room = jnp.minimum(giver - 1, most - taker)
    moved = jax.random.randint(jax.random.fold_in(stream_key, 1), (couples,), 0, 1 << 20) % (room + 1)
    tallies = tallies.at[1:1 + 2 * couples:2].set(giver - moved).at[2:2 + 2 * couples:2].set(taker + moved)
    return tallies[jax.random.permutation(jax.random.fold_in(stream_key, 2), number_of)]


def routed_block(key, own, number, rows, amount, top, limit, lean):
    sequence = jax.random.permutation(key, amount)
    heavy_load, common = portions_of(amount, rows * top, limit, lean, True), portions_of(amount, rows * top, limit, lean, False)
    places = jnp.arange(amount)

    def named(sizes, turn):
        used = int((sizes > 0).sum())
        fixed = max(1, used // 4)
        passed = fixed + (places - fixed + turn * (used - fixed)) % max(1, amount - fixed)
        return jnp.zeros((amount,), jnp.int32).at[sequence[jnp.where(places < fixed, places, passed)]].set(jnp.asarray(sizes, jnp.int32))

    sizes = jnp.where(number % 4 == 0, named(heavy_load, number // 4), named(common, number - number // 4 - 1))
    mixed = jax.random.permutation(jax.random.fold_in(own, 3), amount)
    donor, sink = mixed[0:amount // 2 * 2:2], mixed[1:amount // 2 * 2:2]
    slack = jnp.minimum(sizes[donor] - 1, limit - sizes[sink]) // 2
    slack = jnp.where((donor == sequence[0]) | (sink == sequence[0]) | (sizes[sink] == 0), 0, jnp.maximum(slack, 0))
    passed = jax.random.randint(jax.random.fold_in(own, 4), (amount // 2,), 0, 1 << 20) % (slack + 1)
    sizes = sizes.at[donor].add(-passed).at[sink].add(passed)
    items = jnp.searchsorted(jnp.cumsum(sizes), jnp.arange(rows * top), side="right").astype(jnp.int32)
    table = items.reshape(top, rows).T
    table = table[jax.random.permutation(jax.random.fold_in(own, 1), rows)]
    turn = jax.random.randint(jax.random.fold_in(own, 2), (rows, 1), 0, top)
    return jnp.take_along_axis(table, (jnp.arange(top)[None, :] + turn) % top, axis=1)


def portions_of(count, total, reach, lean, full):
    weights = [(1 << 20) // math.isqrt(rank ** lean) + 1 for rank in range(1, count + 1)]
    largest = reach if full else min(reach, max(-(-total // count), total * weights[0] // sum(weights)))
    least = 1 if total - largest >= count - 1 else 0
    counts, surplus = [largest] + [least] * (count - 1), total - largest - least * (count - 1)
    while surplus > 0:
        movable = [i for i in range(1, count) if counts[i] < largest] or [i for i in range(1, count) if counts[i] < reach]
        whole, remaining = sum([weights[i] for i in movable]), surplus
        for i in movable:
            more = min(reach - counts[i], max(1, remaining * weights[i] // whole), surplus)
            counts[i] = counts[i] + more
            surplus = surplus - more
    return np.array(counts)


def scatter_about(stream_key, shape, scale, limit, cuts=(), kind=jnp.bfloat16):
    gain = block_scale(stream_key, shape, cuts, -0.22, 0.18) if cuts else 1.0
    entries = jax.random.normal(stream_key, shape, jnp.float32) * scale * gain
    return jnp.minimum(jnp.maximum(entries, -limit), limit).astype(kind)


def setup_inputs(seed: int = 0) -> dict:
    splits = jax.random.split(jax.random.key(seed), 9)
    queries = draw_queries(jax.random.fold_in(splits[8], 71), 0)
    prompt_prefix_keys = draw_prompt_prefix_keys(jax.random.fold_in(splits[8], 71), 0)
    prompt_prefix_values = scatter_about(splits[2], (PREFIX_TOKENS, KEY_VALUE_HEADS * HEAD_WIDTH), 1.0, 6.0, ((0, 16), (1, 8)))
    continuation_keys = draw_continuation_keys(jax.random.fold_in(splits[8], 71), 0)
    continuation_values = scatter_about(splits[4], (TOKEN_SLOTS, KEY_VALUE_HEADS * HEAD_WIDTH), 1.0, 6.0, ((0, 16), (1, 8)))
    owners_keys = jax.random.split(jax.random.fold_in(splits[5], 1), BRANCH_TOTAL // BR_DEV)
    owners_turns = jax.random.permutation(jax.random.fold_in(splits[5], 3), BRANCH_TOTAL // BR_DEV)
    owners = jax.vmap(lambda own, number: routed_block(jax.random.fold_in(splits[5], 2), own, number, BR_DEV, N_SEQ, FAN, CAP, 2))(owners_keys, owners_turns).reshape((BRANCH_TOTAL, FAN))
    lengths = ragged(splits[6], BRANCH_TOTAL, BRANCH_TOTAL * SUFFIX_SLOTS * 5 // 8, SUFFIX_SLOTS, 1).astype(jnp.int32)
    out_weight = scatter_about(splits[7], (QUERY_HEADS * HEAD_WIDTH, D), (16.0 / (QUERY_HEADS * HEAD_WIDTH) ** 0.5), 2.5, ((0, 8),))
    return dict(queries=queries, prompt_prefix_keys=prompt_prefix_keys, prompt_prefix_values=prompt_prefix_values, continuation_keys=continuation_keys, continuation_values=continuation_values, owners=owners, lengths=lengths, out_weight=out_weight)


MASKED_SCORE = -1e30


def attend(query_tile_rows, keys, value_rows, allowed):
    scores = jnp.einsum('thgd,shd->hgts', query_tile_rows.astype(jnp.float32), keys.astype(jnp.float32)) * (HEAD_WIDTH ** -0.5)
    scores = jnp.where(allowed, scores, MASKED_SCORE)
    top = jnp.max(scores, axis=-1, keepdims=True)
    prob = jnp.exp(scores - top)
    total = jnp.sum(prob, axis=-1, keepdims=True)
    weights = lax.optimization_barrier(prob.astype(jnp.bfloat16)).astype(jnp.float32)
    result = jnp.einsum('hgts,shd->thgd', weights, value_rows.astype(jnp.float32)) / jnp.transpose(total, (2, 0, 1, 3))
    return result, top[..., 0] + jnp.log(total[..., 0])


def reference(queries, prompt_prefix_keys, prompt_prefix_values, continuation_keys, continuation_values, owners, lengths, out_weight):
    group_size = QUERY_HEADS // KEY_VALUE_HEADS
    positions = jnp.arange(SUFFIX_SLOTS, dtype=jnp.int32)
    causal = positions[None, :] <= positions[:, None]

    def one_branch(branch):
        first_position = (branch * SUFFIX_SLOTS).astype(jnp.int32)
        query_tile_rows = lax.dynamic_slice_in_dim(queries, first_position, SUFFIX_SLOTS, 0).reshape(SUFFIX_SLOTS, KEY_VALUE_HEADS, group_size, HEAD_WIDTH)
        branch_own_keys = lax.dynamic_slice_in_dim(continuation_keys, first_position, SUFFIX_SLOTS, 0).reshape(SUFFIX_SLOTS, KEY_VALUE_HEADS, HEAD_WIDTH)
        branch_own_values = lax.dynamic_slice_in_dim(continuation_values, first_position, SUFFIX_SLOTS, 0).reshape(SUFFIX_SLOTS, KEY_VALUE_HEADS, HEAD_WIDTH)
        allowed = causal & (positions[None, :] < lengths[branch])
        own_out, own_lse = attend(query_tile_rows, branch_own_keys, branch_own_values, allowed)
        outputs = [own_out]
        lses = [own_lse]
        for slot in range(FAN):
            anchor_point = (owners[branch, slot] * PREFIX_PER_OWNER).astype(jnp.int32)
            shared_pool_keys = lax.dynamic_slice_in_dim(prompt_prefix_keys, anchor_point, PREFIX_PER_OWNER, 0).reshape(PREFIX_PER_OWNER, KEY_VALUE_HEADS, HEAD_WIDTH)
            shared_pool_values = lax.dynamic_slice_in_dim(prompt_prefix_values, anchor_point, PREFIX_PER_OWNER, 0).reshape(PREFIX_PER_OWNER, KEY_VALUE_HEADS, HEAD_WIDTH)
            pool_out, pool_lse = attend(query_tile_rows, shared_pool_keys, shared_pool_values, True)
            outputs.append(lax.optimization_barrier(pool_out.astype(jnp.bfloat16)).astype(jnp.float32))
            lses.append(pool_lse)
        lse_stack = jnp.stack(lses)
        out_stack = jnp.stack(outputs)
        peak = jnp.max(lse_stack, axis=0)
        scale = jnp.exp(lse_stack - peak[None])
        denom = jnp.sum(scale, axis=0)
        numer = jnp.sum(out_stack * jnp.transpose(scale, (0, 3, 1, 2))[..., None], axis=0)
        merged = numer / jnp.transpose(denom, (2, 0, 1))[..., None]
        return merged.reshape(SUFFIX_SLOTS, QUERY_HEADS * HEAD_WIDTH).astype(jnp.bfloat16)

    attention = lax.map(one_branch, jnp.arange(BRANCH_TOTAL, dtype=jnp.int32)).reshape(TOKEN_SLOTS, QUERY_HEADS * HEAD_WIDTH)
    return jnp.dot(attention, out_weight, preferred_element_type=jnp.float32).astype(jnp.bfloat16)
```

```python
import functools

import jax
import jax.numpy as jnp
from jax import lax
from jax.experimental import pallas as pl
from jax.experimental.pallas import tpu as pltpu
from jax.sharding import PartitionSpec as P

HEAD = 128
SLOTS = 32
BRANCHES = 4
FAN = 4
HEADS = 8
COLS = HEADS * SLOTS
HALF = 1024
STRIP = 512
CHUNKS = 8
LOG2E = 1.4426950408889634
SCALE = HEAD**-0.5 * LOG2E
LOW = -1e30
MESH = pl.DeviceIdType.MESH
NT = (((1,), (1,)), ((), ()))
NN = (((1,), (0,)), ((), ()))


def dot(a, b, dims):
    return lax.dot_general(a, b, dims, preferred_element_type=jnp.float32)


def await_bytes(ref, sem):
    pltpu.make_async_copy(ref, ref, sem).wait()


def kernel(
    q_hbm, k_hbm, v_hbm, ck_ref, cv_ref, owners_ref, lengths_ref, w_hbm,
    out_ref,
    w_buf, kp, vp, v_own, qbuf, qs, own_vec, own_buf, raw, tab, inv,
    s_a, s_b, m_ref, l_ref, acc, own_m, own_l, own_acc,
    ret, ret_lse, back, back_lse, attn,
    part, total, pair_send, pair_recv, d_send, d_recv, r_send, r_recv,
    loc_sem, q_ssem, q_rsem, o_ssem, o_rsem, kv_ssem, kv_rsem,
    ret_ssem, ret_rsem, pair_ssem, pair_rsem, d_ssem, d_rsem, r_ssem, r_rsem,
):
    seq = lax.axis_index("seq")
    tp = lax.axis_index("tp")
    y, z = lax.div(seq, 4), lax.rem(seq, 4)
    x, core = lax.div(tp, 2), lax.rem(tp, 2)
    kv_pos = (1 - core) * z + core * y
    q_pos = (1 - core) * y + core * z

    def kv_seq(step):
        a = lax.rem(kv_pos + step, 4)
        return (1 - core) * (q_pos * 4 + a) + core * (a * 4 + q_pos)

    def q_seq(step):
        a = lax.rem(q_pos + step, 4)
        return (1 - core) * (a * 4 + kv_pos) + core * (kv_pos * 4 + a)

    kv_right, kv_left = (kv_seq(1), tp), (kv_seq(3), tp)
    peers = {1: (q_seq(3), tp), 2: (q_seq(1), tp), 3: (q_seq(2), tp)}
    mirror = {1: 2, 2: 1, 3: 3}
    partner = (seq, x * 2 + 1 - core)
    x_right = (seq, lax.rem(x + 1, 4) * 2 + core)
    x_left = (seq, lax.rem(x + 3, 4) * 2 + core)
    everyone = (kv_right, kv_left, peers[1], peers[2], peers[3], partner, x_right, x_left)

    def remote(src, dst, ssem, rsem, device):
        return pltpu.make_async_remote_copy(
            src_ref=src, dst_ref=dst, send_sem=ssem, recv_sem=rsem, device_id=device, device_id_type=MESH
        )

    barrier = pltpu.get_barrier_semaphore()
    for device in everyone:
        pl.semaphore_signal(barrier, inc=1, device_id=device, device_id_type=MESH)

    copy_v = pltpu.make_async_copy(v_hbm, v_own, loc_sem.at[0])
    copy_v.start()
    copy_q = pltpu.make_async_copy(q_hbm, qbuf.at[0], q_rsem.at[0])
    copy_q.start()
    copy_k = [
        pltpu.make_async_copy(k_hbm.at[pl.ds(h * HALF, HALF), :], kp.at[h], loc_sem.at[1 + h]) for h in range(2)
    ]
    for c in copy_k:
        c.start()

    rows = lax.broadcasted_iota(jnp.int32, (8, 128), 0)
    lanes = lax.broadcasted_iota(jnp.int32, (8, 128), 1)
    vec = jnp.zeros((8, 128), jnp.int32)
    for b in range(BRANCHES):
        for f in range(FAN):
            vec = jnp.where((rows == b) & (lanes == f), owners_ref[b, f], vec)
    own_vec[...] = vec
    copy_o = pltpu.make_async_copy(own_vec, own_buf.at[0], o_rsem.at[0])
    copy_o.start()

    pl.semaphore_wait(barrier, len(everyone))

    sends = []
    for j in (3, 1, 2):
        sends.append(remote(own_vec, own_buf.at[mirror[j]], o_ssem.at[j], o_rsem.at[mirror[j]], peers[j]))
        sends[-1].start()
    for j in (1, 2, 3):
        sends.append(remote(q_hbm, qbuf.at[mirror[j]], q_ssem.at[j], q_rsem.at[mirror[j]], peers[j]))
        sends[-1].start()
    routes = ((0, 2, kv_right), (1, 3, kv_left), (1, 4, kv_right), (0, 5, kv_left))

    def kv_send(h, piece, device, which):
        src, dst = (kp, kp) if which == 0 else (vp, vp)
        return remote(src.at[h], dst.at[piece], kv_ssem.at[which, piece], kv_rsem.at[which, piece], device)

    for c in copy_k:
        c.wait()
    for h, piece, device in routes[:2]:
        sends.append(kv_send(h, piece, device, 0))
        sends[-1].start()
    copy_v.wait()
    for h in range(2):
        vp[h] = jnp.transpose(v_own[pl.ds(h * HALF, HALF), :].astype(jnp.float32)).astype(jnp.bfloat16)
    for h, piece, device in routes[:2]:
        sends.append(kv_send(h, piece, device, 1))
        sends[-1].start()
    for which in range(2):
        for h, piece, device in routes[2:]:
            sends.append(kv_send(h, piece, device, which))
            sends[-1].start()
    copy_w = pltpu.make_async_copy(w_hbm, w_buf, loc_sem.at[3])
    copy_w.start()

    m_ref[...] = jnp.full(m_ref.shape, LOW, jnp.float32)
    l_ref[...] = jnp.zeros(l_ref.shape, jnp.float32)
    acc[...] = jnp.zeros(acc.shape, jnp.float32)

    def slot_of(o, j, k):
        return o * 8 + j * 2 + k

    def column_max(scores):
        return jnp.max(scores.reshape(scores.shape[0] // 64, 64, COLS), axis=0)

    def advance(ahead, dst, behind, src, top):
        if ahead is not None:
            piece, o, j, k = ahead
            q_now = qs[j * BRANCHES + tab[slot_of(o, j, k)]]
        if behind is not None:
            piece2, o2, j2, k2 = behind
            s2 = slot_of(o2, j2, k2)
            old = m_ref[s2]
            new = jnp.maximum(old, top)
            shrink = jnp.exp2(old - new)
        best = gain = None
        for c in range(HALF // STRIP):
            span = pl.ds(c * STRIP, STRIP)
            if ahead is not None:
                k_now = kp[piece, span, :]
                scores = dot(jnp.concatenate([k_now, k_now], axis=1), q_now, NT)
            if behind is not None:
                weights = jnp.exp2(src[span, :] - new).astype(jnp.bfloat16)
            if ahead is not None:
                dst[span, :] = scores
                here = column_max(scores)
                best = here if best is None else jnp.maximum(best, here)
            if behind is not None:
                values = jnp.concatenate([vp[piece2, :, span], jnp.ones((16, STRIP), jnp.bfloat16)], axis=0)
                term = dot(values, weights, NN)
                gain = term if gain is None else gain + term
        if behind is not None:
            m_ref[s2] = new
            l_ref[s2] = l_ref[s2] * shrink + gain[HEAD : HEAD + 1]
            acc[s2] = acc[s2] * shrink + gain[:HEAD]
        if ahead is not None:
            return jnp.max(best, axis=0, keepdims=True)

    def four(j, o, first_piece):
        steps = [(first_piece + h, o, j, k) for h in range(2) for k in range(2)]
        bufs = (s_a, s_b)
        top = advance(steps[0], bufs[0], None, None, None)
        for t in range(4):
            ahead = steps[t + 1] if t < 3 else None
            top = advance(ahead, bufs[(t + 1) % 2], steps[t], bufs[t % 2], top)

    group = [seq, kv_seq(3), kv_seq(1), kv_seq(2)]

    def source(j, carry):
        await_bytes(own_buf.at[j], o_rsem.at[j])
        copy = pltpu.make_async_copy(own_buf.at[j], raw, loc_sem.at[4])
        copy.start()
        copy.wait()
        for o in range(4):
            count, first, second = jnp.int32(0), jnp.int32(0), jnp.int32(0)
            for b in range(BRANCHES):
                hit = raw[b, 0] == group[o]
                for f in range(1, FAN):
                    hit = hit | (raw[b, f] == group[o])
                inv[(o * 4 + j) * BRANCHES + b] = jnp.where(hit & (count < 2), count, -1)
                first = jnp.where(hit & (count == 0), b, first)
                second = jnp.where(hit & (count == 1), b, second)
                count = count + hit.astype(jnp.int32)
            tab[slot_of(o, j, 0)] = first
            tab[slot_of(o, j, 1)] = second
        await_bytes(qbuf.at[j], q_rsem.at[j])
        for b in range(BRANCHES):
            stacked = jnp.concatenate([qbuf[j, b, :, pl.ds(h * HEAD, HEAD)] for h in range(HEADS)], axis=0)
            exact = stacked.astype(jnp.float32) * SCALE
            high = exact.astype(jnp.bfloat16)
            qs[j * BRANCHES + b, :, :HEAD] = high
            qs[j * BRANCHES + b, :, HEAD:] = (exact - high.astype(jnp.float32)).astype(jnp.bfloat16)
        four(j, 0, 0)
        return carry

    lax.fori_loop(0, 4, source, 0)

    row = lax.broadcasted_iota(jnp.int32, (BRANCHES * SLOTS, COLS), 0)
    slot = lax.rem(lax.broadcasted_iota(jnp.int32, (BRANCHES * SLOTS, COLS), 1), SLOTS)
    ck = ck_ref[...]
    ck2 = jnp.concatenate([ck, ck], axis=1)
    cv_t = jnp.transpose(cv_ref[...].astype(jnp.float32)).astype(jnp.bfloat16)
    for b in range(BRANCHES):
        key = row - b * SLOTS
        allowed = (key >= 0) & (key <= slot) & (key < lengths_ref[b])
        scores = jnp.where(allowed, dot(ck2, qs[b], NT), LOW)
        top = jnp.max(scores, axis=0, keepdims=True)
        prob = jnp.where(allowed, jnp.exp2(scores - top), 0.0)
        own_m[b] = top
        own_l[b] = jnp.sum(prob, axis=0, keepdims=True)
        own_acc[b] = dot(cv_t, prob.astype(jnp.bfloat16), NN)

    for d in range(2):
        for piece in (2 + 2 * d, 3 + 2 * d):
            for which, buf in ((0, kp), (1, vp)):
                await_bytes(buf.at[piece], kv_rsem.at[which, piece])
                if d == 0:
                    sends.append(kv_send(piece, piece + 4, kv_right if piece == 2 else kv_left, which))
                    sends[-1].start()

        def step_of(t, d=d):
            return (2 + 2 * d + lax.div(t, 8), 1 + lax.div(t, 8), lax.div(lax.rem(t, 8), 2), lax.rem(t, 2))

        def two(i, top, step_of=step_of):
            t = 2 * i
            top = advance(step_of(t + 1), s_b, step_of(t), s_a, top)
            return advance(step_of(lax.rem(t + 2, 16)), s_a, step_of(t + 1), s_b, top)

        lax.fori_loop(0, 8, two, advance(step_of(jnp.int32(0)), s_a, None, None, None))

    for piece in (6, 7):
        for which, buf in ((0, kp), (1, vp)):
            await_bytes(buf.at[piece], kv_rsem.at[which, piece])

    def ret_copies(j):
        return (
            remote(ret.at[j], back.at[mirror[j]], ret_ssem.at[0, j], ret_rsem.at[0, mirror[j]], peers[j]),
            remote(ret_lse.at[j], back_lse.at[mirror[j]], ret_ssem.at[1, j], ret_rsem.at[1, mirror[j]], peers[j]),
        )

    def finish(i, carry):
        j = 3 - i
        four(j, 3, 6)
        for b in range(BRANCHES):
            slots, tops, sums, oks = [], [], [], []
            for o in range(4):
                place = inv[(o * 4 + j) * BRANCHES + b]
                ok = place >= 0
                s = slot_of(o, j, jnp.where(ok, place, 0))
                slots.append(s)
                oks.append(ok)
                tops.append(jnp.where(ok, m_ref[s], LOW))
                sums.append(l_ref[s])
            peak = functools.reduce(jnp.maximum, tops)
            scales = [jnp.where(ok, jnp.exp2(t - peak), 0.0) for ok, t in zip(oks, tops)]
            denom = sum(a * l for a, l in zip(scales, sums))
            any_ok = denom > 0.0
            safe = jnp.where(any_ok, denom, 1.0)
            merged = sum(acc[s] * (a / safe) for s, a in zip(slots, scales))
            ret[j, b] = merged.astype(jnp.bfloat16)
            ret_lse[j, b : b + 1, :] = jnp.where(any_ok, peak + jnp.log(safe) * LOG2E, LOW)
        for n in (1, 2, 3):

            @pl.when(j == n)
            def _():
                for c in ret_copies(n):
                    c.start()

        return carry

    lax.fori_loop(0, 4, finish, 0)
    for n in (1, 2, 3):
        for c in ret_copies(n):
            c.wait_recv()

    for b in range(BRANCHES):
        lses = [own_m[b] + jnp.log(own_l[b]) * LOG2E, ret_lse[0, b : b + 1, :]]
        lses += [back_lse[n, b : b + 1, :] for n in (1, 2, 3)]
        peak = functools.reduce(jnp.maximum, lses)
        scales = [jnp.exp2(t - peak) for t in lses]
        denom = sum(scales)
        merged = own_acc[b] * (scales[0] / (denom * own_l[b]))
        outs = [ret[0, b]] + [back[n, b] for n in (1, 2, 3)]
        for a, o in zip(scales[1:], outs):
            merged = merged + o.astype(jnp.float32) * (a / denom)
        turned = jnp.transpose(merged).astype(jnp.bfloat16)
        for h in range(HEADS):
            attn[b * SLOTS : (b + 1) * SLOTS, h * HEAD : (h + 1) * HEAD] = turned[h * SLOTS : (h + 1) * SLOTS, :]
    copy_w.wait()

    width = w_buf.shape[1] // CHUNKS
    mid = width // 2
    share = part.shape[2]
    right, left, far = lax.rem(x + 1, 4), lax.rem(x + 3, 4), lax.rem(x + 2, 4)

    def pair_copy(n):
        return remote(pair_send.at[n], pair_recv.at[n], pair_ssem.at[n], pair_rsem.at[n], partner)

    def d_copies(n):
        return tuple(
            remote(d_send.at[n, i], d_recv.at[n, i], d_ssem.at[n, i], d_rsem.at[n, i], device)
            for i, device in ((0, x_right), (1, x_left))
        )

    def r_copies(n):
        return tuple(
            remote(r_send.at[n, i], r_recv.at[n, i], r_ssem.at[n, i], r_rsem.at[n, i], device)
            for i, device in ((0, x_right), (1, x_left))
        )

    def project(n):
        columns = pl.ds(pl.multiple_of(n * width, width), width)
        part[n] = dot(attn[...], w_buf[:, columns], NN).reshape(8, share, width)
        for i in range(4):
            pair_send[n, i] = part[n, 2 * i + 1 - core].astype(jnp.bfloat16)
        pair_copy(n).start()

    def pair_sum(n):
        pair_copy(n).wait_recv()
        for i in range(4):
            total[n, i] = part[n, 2 * i + core] + pair_recv[n, i].astype(jnp.float32)
        d_send[n, 0] = total[n, far, :, :mid].astype(jnp.bfloat16)
        d_send[n, 1] = total[n, far, :, mid:].astype(jnp.bfloat16)
        for c in d_copies(n):
            c.start()

    def ring_sum(n):
        for c in d_copies(n):
            c.wait_recv()
        r_send[n, 0, :, :mid] = (total[n, right, :, :mid] + d_recv[n, 0].astype(jnp.float32)).astype(jnp.bfloat16)
        r_send[n, 0, :, mid:] = total[n, right, :, mid:].astype(jnp.bfloat16)
        r_send[n, 1, :, :mid] = total[n, left, :, :mid].astype(jnp.bfloat16)
        r_send[n, 1, :, mid:] = (total[n, left, :, mid:] + d_recv[n, 1].astype(jnp.float32)).astype(jnp.bfloat16)
        for c in r_copies(n):
            c.start()

    def last_sum(n):
        for c in r_copies(n):
            c.wait_recv()
        columns = pl.ds(pl.multiple_of(n * width, width), width)
        out_ref[:, columns] = (
            total[n, x] + r_recv[n, 0].astype(jnp.float32) + r_recv[n, 1].astype(jnp.float32)
        ).astype(jnp.bfloat16)

    def tail(i, carry):
        for lag, stage in enumerate((project, pair_sum, ring_sum, last_sum)):
            n = i - lag

            @pl.when((n >= 0) & (n < CHUNKS))
            def _():
                stage(n)

        return carry

    lax.fori_loop(0, CHUNKS + 3, tail, 0)

    for c in sends:
        c.wait_send()
    for n in (1, 2, 3):
        for c in ret_copies(n):
            c.wait_send()

    def drain(n, carry):
        pair_copy(n).wait_send()
        for c in d_copies(n) + r_copies(n):
            c.wait_send()
        return carry

    lax.fori_loop(0, CHUNKS, drain, 0)


def body(queries, keys, values, own_keys, own_values, owners, lengths, out_weight):
    share = queries.shape[0] // 8
    depth, columns = out_weight.shape
    width = columns // CHUNKS
    mid = width // 2
    bf16, f32, i32 = jnp.bfloat16, jnp.float32, jnp.int32
    vmem = pltpu.VMEM
    dma = pltpu.SemaphoreType.DMA
    anywhere = pl.BlockSpec(memory_space=pl.ANY)
    inside = pl.BlockSpec(memory_space=pltpu.VMEM)
    scalars = pl.BlockSpec(memory_space=pltpu.SMEM)
    return pl.pallas_call(
        kernel,
        out_shape=jax.ShapeDtypeStruct((share, columns), bf16),
        in_specs=[anywhere, anywhere, anywhere, inside, inside, scalars, scalars, anywhere],
        out_specs=inside,
        scratch_shapes=[
            vmem((depth, columns), bf16),
            vmem((8, HALF, HEAD), bf16),
            vmem((8, HEAD, HALF), bf16),
            vmem((2 * HALF, HEAD), bf16),
            vmem((4, BRANCHES, SLOTS, HEADS * HEAD), bf16),
            vmem((4 * BRANCHES, COLS, 2 * HEAD), bf16),
            vmem((8, 128), i32),
            vmem((4, 8, 128), i32),
            pltpu.SMEM((8, 128), i32),
            pltpu.SMEM((32,), i32),
            pltpu.SMEM((64,), i32),
            vmem((HALF, COLS), f32),
            vmem((HALF, COLS), f32),
            vmem((32, 1, COLS), f32),
            vmem((32, 1, COLS), f32),
            vmem((32, HEAD, COLS), f32),
            vmem((BRANCHES, 1, COLS), f32),
            vmem((BRANCHES, 1, COLS), f32),
            vmem((BRANCHES, HEAD, COLS), f32),
            vmem((4, BRANCHES, HEAD, COLS), bf16),
            vmem((4, 8, COLS), f32),
            vmem((4, BRANCHES, HEAD, COLS), bf16),
            vmem((4, 8, COLS), f32),
            vmem((BRANCHES * SLOTS, depth), bf16),
            vmem((CHUNKS, 8, share, width), f32),
            vmem((CHUNKS, 4, share, width), f32),
            vmem((CHUNKS, 4, share, width), bf16),
            vmem((CHUNKS, 4, share, width), bf16),
            vmem((CHUNKS, 2, share, mid), bf16),
            vmem((CHUNKS, 2, share, mid), bf16),
            vmem((CHUNKS, 2, share, width), bf16),
            vmem((CHUNKS, 2, share, width), bf16),
            dma((5,)),
            dma((4,)), dma((4,)), dma((4,)), dma((4,)),
            dma((2, 8)), dma((2, 8)),
            dma((2, 4)), dma((2, 4)),
            dma((CHUNKS,)), dma((CHUNKS,)),
            dma((CHUNKS, 2)), dma((CHUNKS, 2)), dma((CHUNKS, 2)), dma((CHUNKS, 2)),
        ],
        compiler_params=pltpu.CompilerParams(
            collective_id=0, has_side_effects=True, vmem_limit_bytes=58 * 1024 * 1024
        ),
        name="branch_attention",
    )(
        queries.reshape(BRANCHES, SLOTS, queries.shape[1]),
        keys, values, own_keys, own_values, owners, lengths, out_weight,
    )


def solution(mesh):
    in_specs = (
        P("seq", "tp"),
        P("seq", "tp"),
        P("seq", "tp"),
        P("seq", "tp"),
        P("seq", "tp"),
        P("seq", None),
        P("seq"),
        P("tp", None),
    )
    out_specs = P(("seq", "tp"), None)
    return jax.shard_map(body, mesh=mesh, in_specs=in_specs, out_specs=out_specs, check_vma=False)
```

```python
import functools

import jax
import jax.numpy as jnp
from jax import lax
from jax.experimental import pallas as pl
from jax.experimental.pallas import tpu as pltpu
from jax.sharding import PartitionSpec as P

HEAD = 128
SLOTS = 32
BRANCHES = 4
FAN = 4
HEADS = 8
COLS = HEADS * SLOTS
HALF = 1024
STRIP = 512
CHUNKS = 4
LAGS = (0, 1, 3, 5)
LOG2E = 1.4426950408889634
SCALE = HEAD**-0.5 * LOG2E
LOW = -1e30
MESH = pl.DeviceIdType.MESH
NT = (((1,), (1,)), ((), ()))
NN = (((1,), (0,)), ((), ()))


def dot(a, b, dims):
    return lax.dot_general(a, b, dims, preferred_element_type=jnp.float32)


def await_bytes(ref, sem):
    pltpu.make_async_copy(ref, ref, sem).wait()


def kernel(
    q_hbm, k_hbm, v_hbm, ck_ref, cv_ref, owners_ref, lengths_ref, w_hbm,
    out_ref,
    w_buf, kp, vp, v_own, qbuf, qs, own_vec, own_buf, raw, tab, inv,
    s_a, s_b, p_a, p_b, m_ref, l_ref, acc, own_m, own_l, own_acc,
    ret, ret_lse, back, back_lse, attn,
    part, total, pair_send, pair_recv, d_send, d_recv, r_send, r_recv,
    loc_sem, q_ssem, q_rsem, o_ssem, o_rsem, kv_ssem, kv_rsem,
    ret_ssem, ret_rsem, pair_ssem, pair_rsem, d_ssem, d_rsem, r_ssem, r_rsem,
):
    seq = lax.axis_index("seq")
    tp = lax.axis_index("tp")
    y, z = lax.div(seq, 4), lax.rem(seq, 4)
    x, core = lax.div(tp, 2), lax.rem(tp, 2)
    kv_pos = (1 - core) * z + core * y
    q_pos = (1 - core) * y + core * z

    def kv_seq(step):
        a = lax.rem(kv_pos + step, 4)
        return (1 - core) * (q_pos * 4 + a) + core * (a * 4 + q_pos)

    def q_seq(step):
        a = lax.rem(q_pos + step, 4)
        return (1 - core) * (a * 4 + kv_pos) + core * (kv_pos * 4 + a)

    kv_right, kv_left = (kv_seq(1), tp), (kv_seq(3), tp)
    peers = {1: (q_seq(3), tp), 2: (q_seq(1), tp), 3: (q_seq(2), tp)}
    mirror = {1: 2, 2: 1, 3: 3}
    partner = (seq, x * 2 + 1 - core)
    x_right = (seq, lax.rem(x + 1, 4) * 2 + core)
    x_left = (seq, lax.rem(x + 3, 4) * 2 + core)
    everyone = (kv_right, kv_left, peers[1], peers[2], peers[3], partner, x_right, x_left)

    def remote(src, dst, ssem, rsem, device):
        return pltpu.make_async_remote_copy(
            src_ref=src, dst_ref=dst, send_sem=ssem, recv_sem=rsem, device_id=device, device_id_type=MESH
        )

    barrier = pltpu.get_barrier_semaphore()
    for device in everyone:
        pl.semaphore_signal(barrier, inc=1, device_id=device, device_id_type=MESH)

    copy_v = pltpu.make_async_copy(v_hbm, v_own, loc_sem.at[0])
    copy_v.start()
    copy_q = pltpu.make_async_copy(q_hbm, qbuf.at[0], q_rsem.at[0])
    copy_q.start()
    copy_k = pltpu.make_async_copy(k_hbm, kp.at[pl.ds(0, 4)], loc_sem.at[1])
    copy_k.start()

    rows = lax.broadcasted_iota(jnp.int32, (8, 128), 0)
    lanes = lax.broadcasted_iota(jnp.int32, (8, 128), 1)
    vec = jnp.zeros((8, 128), jnp.int32)
    for b in range(BRANCHES):
        for f in range(FAN):
            vec = jnp.where((rows == b) & (lanes == f), owners_ref[b, f], vec)
    own_vec[...] = vec
    copy_o = pltpu.make_async_copy(own_vec, own_buf.at[0], o_rsem.at[0])
    copy_o.start()

    copy_v.wait()
    for n in (0, 2, 1, 3):
        vp[n] = jnp.transpose(v_own[pl.ds(n * STRIP, STRIP), :].astype(jnp.float32)).astype(jnp.bfloat16)
    pl.semaphore_wait(barrier, len(everyone))

    sends = []
    for j in (3, 1, 2):
        sends.append(remote(own_vec, own_buf.at[mirror[j]], o_ssem.at[j], o_rsem.at[mirror[j]], peers[j]))
        sends[-1].start()
    for j in (1, 2):
        sends.append(remote(q_hbm, qbuf.at[mirror[j]], q_ssem.at[j], q_rsem.at[mirror[j]], peers[j]))
        sends[-1].start()
    q_relay = [
        remote(qbuf.at[1, pl.ds(0, 2)], qbuf.at[3, pl.ds(0, 2)], q_ssem.at[3], q_rsem.at[3], peers[2]),
        remote(qbuf.at[2, pl.ds(2, 2)], qbuf.at[3, pl.ds(2, 2)], q_ssem.at[4], q_rsem.at[4], peers[1]),
    ]

    def kv_send(src, dst, count, device, which):
        buf = (kp, vp)[which]
        source_ref = k_hbm if which == 0 and src < 4 else buf
        return remote(
            source_ref.at[pl.ds(src, count)], buf.at[pl.ds(dst, count)],
            kv_ssem.at[which, dst], kv_rsem.at[which, dst], device,
        )

    def kv_await(quarter, count):
        for which, buf in ((0, kp), (1, vp)):
            await_bytes(buf.at[pl.ds(quarter, count)], kv_rsem.at[which, quarter])

    opening = [
        [kv_send(i, 4 + i, 1, kv_right, which) for which in range(2)]
        + [kv_send(2 + i, 6 + i, 1, kv_left, which) for which in range(2)]
        for i in range(2)
    ]
    closing = [
        kv_send(src, dst, 2, device, which)
        for which in range(2) for src, dst, device in ((2, 8, kv_right), (0, 10, kv_left))
    ]
    relay = [
        [kv_send(4 + i, 12 + i, 1, kv_right, which) for which in range(2)]
        + [kv_send(6 + i, 14 + i, 1, kv_left, which) for which in range(2)]
        for i in range(2)
    ]
    sends += q_relay + opening[0] + opening[1] + closing + relay[0] + relay[1]

    copy_k.wait()
    copy_w = pltpu.make_async_copy(w_hbm, w_buf, loc_sem.at[2])
    copy_w.start()

    m_ref[...] = jnp.full(m_ref.shape, LOW, jnp.float32)
    l_ref[...] = jnp.zeros(l_ref.shape, jnp.float32)
    acc[...] = jnp.zeros(acc.shape, jnp.float32)

    def slot_of(o, j, k):
        return o * 8 + j * 2 + k

    def stage(ahead, s_out, middle, top, s_in, p_out, behind, shrink, p_in):
        best = gain = next_shrink = None
        if ahead is not None:
            quarter, gap, j, s0 = ahead
            q_now = qs[j * BRANCHES + tab[s0]]
        if middle is not None:
            mid_slot = middle[3]
            old = m_ref[mid_slot]
            new = jnp.maximum(old, jnp.max(top, axis=0, keepdims=True))
            next_shrink = jnp.exp2(old - new)
            m_ref[mid_slot] = new
        for c in range(2):
            span = pl.ds(c * STRIP, STRIP)
            if ahead is not None:
                k_now = kp[quarter + c * gap]
                scores = dot(jnp.concatenate([k_now, k_now], axis=1), q_now, NT)
            if behind is not None:
                values = jnp.concatenate([vp[behind[0] + c * behind[1]], jnp.ones((16, STRIP), jnp.bfloat16)], axis=0)
                term = dot(values, p_in[span, :], NN)
                gain = term if gain is None else gain + term
            if middle is not None:
                p_out[span, :] = jnp.exp2(s_in[span, :] - new).astype(jnp.bfloat16)
            if ahead is not None:
                s_out[span, :] = scores
                here = jnp.max(scores.reshape(STRIP // 64, 64, COLS), axis=0)
                best = here if best is None else jnp.maximum(best, here)
        if behind is not None:
            s2 = behind[3]
            l_ref[s2] = l_ref[s2] * shrink + gain[HEAD : HEAD + 1]
            acc[s2] = acc[s2] * shrink + gain[:HEAD]
        if best is not None:
            best = jnp.max(best.reshape(8, 8, COLS), axis=0)
        return best, next_shrink

    def step_of(i, u):
        own = 1 - lax.div(i + (6 if u < 4 else 7), 8)
        piece = (1 - own) * (i - (2 if u < 4 else 1))
        far = lax.div(piece, 4)
        quarter = own * 2 * (u % 4 // 2) + (1 - own) * (4 + 2 * piece)
        owner = (1 - own) * ((1 - far) * (1 + lax.rem(piece, 2)) + 3 * far)
        j = own * (2 * i + (1 if u < 4 else 2)) + (1 - own) * ((2 if u < 4 else 0) + u % 4 // 2)
        return quarter, 1 + far, j, slot_of(owner, j, u % 2)

    def last_step(u):
        return 13, 2, 3 - u // 2, slot_of(3, 3 - u // 2, u % 2)

    scores_of, probs_of = (s_a, s_b), (p_a, p_b)

    def advance(u, ahead, middle, behind, top, shrink):
        return stage(
            ahead, scores_of[u % 2], middle, top, scores_of[(u + 1) % 2], probs_of[(u + 1) % 2],
            behind, shrink, probs_of[u % 2],
        )

    group = [seq, kv_seq(3), kv_seq(1), kv_seq(2)]

    def own_rows():
        row = lax.broadcasted_iota(jnp.int32, (BRANCHES * SLOTS, COLS), 0)
        slot = lax.rem(lax.broadcasted_iota(jnp.int32, (BRANCHES * SLOTS, COLS), 1), SLOTS)
        ck = ck_ref[...]
        ck2 = jnp.concatenate([ck, ck], axis=1)
        cv_t = jnp.transpose(cv_ref[...].astype(jnp.float32)).astype(jnp.bfloat16)
        for b in range(BRANCHES):
            key = row - b * SLOTS
            allowed = (key >= 0) & (key <= slot) & (key < lengths_ref[b])
            scores = jnp.where(allowed, dot(ck2, qs[b], NT), LOW)
            top = jnp.max(scores, axis=0, keepdims=True)
            prob = jnp.where(allowed, jnp.exp2(scores - top), 0.0)
            own_m[b] = top
            own_l[b] = jnp.sum(prob, axis=0, keepdims=True)
            own_acc[b] = dot(cv_t, prob.astype(jnp.bfloat16), NN)

    def pass_on(n):
        for quarter, base in ((4 + n, 0), (6 + n, 2)):
            kv_await(quarter, 1)
            for c in relay[n][base : base + 2]:
                c.start()

    def find_slots(j, carry):
        await_bytes(own_buf.at[j], o_rsem.at[j])
        copy = pltpu.make_async_copy(own_buf.at[j], raw, loc_sem.at[3])
        copy.start()
        copy.wait()
        for o in range(4):
            count, first, second = jnp.int32(0), jnp.int32(0), jnp.int32(0)
            for b in range(BRANCHES):
                hit = raw[b, 0] == group[o]
                for f in range(1, FAN):
                    hit = hit | (raw[b, f] == group[o])
                inv[(o * 4 + j) * BRANCHES + b] = jnp.where(hit & (count < 2), count, -1)
                first = jnp.where(hit & (count == 0), b, first)
                second = jnp.where(hit & (count == 1), b, second)
                count = count + hit.astype(jnp.int32)
            tab[slot_of(o, j, 0)] = first
            tab[slot_of(o, j, 1)] = second
        return carry

    def split_queries(j, carry):
        for b in range(BRANCHES):
            stacked = jnp.concatenate([qbuf[j, b, :, pl.ds(h * HEAD, HEAD)] for h in range(HEADS)], axis=0)
            exact = stacked.astype(jnp.float32) * SCALE
            high = exact.astype(jnp.bfloat16)
            qs[j * BRANCHES + b, :, :HEAD] = high
            qs[j * BRANCHES + b, :, HEAD:] = (exact - high.astype(jnp.float32)).astype(jnp.bfloat16)
        return carry

    def attend_round(i, carry):
        top, shrink = carry

        @pl.when(i == 0)
        def _():
            for n in (1, 2):
                await_bytes(qbuf.at[n], q_rsem.at[n])
                q_relay[n - 1].start()
            for c in closing:
                c.start()

        @pl.when(i == 1)
        def _():
            pass_on(0)
            await_bytes(qbuf.at[3, pl.ds(0, 2)], q_rsem.at[3])
            await_bytes(qbuf.at[3, pl.ds(2, 2)], q_rsem.at[4])
            pass_on(1)

        @pl.when(i < 2)
        def _():
            lax.fori_loop(1 + 2 * i, 3 + i, split_queries, 0)

        for n, quarter, count in ((3, 8, 2), (4, 10, 2), (5, 12, 1), (5, 14, 1)):

            @pl.when(i == n)
            def _():
                kv_await(quarter, count)

        for u in range(8):
            middle = step_of(i, u - 1) if u >= 1 else step_of(i - 1, 7)
            behind = step_of(i, u - 2) if u >= 2 else step_of(i - 1, 6 + u)
            top, shrink = advance(u, step_of(i, u), middle, behind, top, shrink)
        return top, shrink

    find_slots(0, 0)
    await_bytes(qbuf.at[0], q_rsem.at[0])
    split_queries(0, 0)
    opened = [step_of(-1, 4 + u) for u in range(4)]
    top = shrink = None
    for u in range(4):
        top, shrink = advance(
            u, opened[u], opened[u - 1] if u >= 1 else None, opened[u - 2] if u >= 2 else None, top, shrink
        )
    for c in opening[0] + opening[1]:
        c.start()
    own_rows()
    lax.fori_loop(1, 4, find_slots, 0)
    top, shrink = lax.fori_loop(0, 6, attend_round, (top, shrink))
    kv_await(13, 1)
    kv_await(15, 1)

    def ret_copies(j):
        return (
            remote(ret.at[j], back.at[mirror[j]], ret_ssem.at[0, j], ret_rsem.at[0, mirror[j]], peers[j]),
            remote(ret_lse.at[j], back_lse.at[mirror[j]], ret_ssem.at[1, j], ret_rsem.at[1, mirror[j]], peers[j]),
        )

    def finish(j):
        for b in range(BRANCHES):
            slots, tops, sums, oks = [], [], [], []
            for o in range(4):
                place = inv[(o * 4 + j) * BRANCHES + b]
                ok = place >= 0
                s = slot_of(o, j, jnp.where(ok, place, 0))
                slots.append(s)
                oks.append(ok)
                tops.append(jnp.where(ok, m_ref[s], LOW))
                sums.append(l_ref[s])
            peak = functools.reduce(jnp.maximum, tops)
            scales = [jnp.where(ok, jnp.exp2(t - peak), 0.0) for ok, t in zip(oks, tops)]
            denom = sum(a * l for a, l in zip(scales, sums))
            any_ok = denom > 0.0
            safe = jnp.where(any_ok, denom, 1.0)
            merged = sum(acc[s] * (a / safe) for s, a in zip(slots, scales))
            ret[j, b] = merged.astype(jnp.bfloat16)
            ret_lse[j, b : b + 1, :] = jnp.where(any_ok, peak + jnp.log(safe) * LOG2E, LOW)
        if j:
            for c in ret_copies(j):
                c.start()

    final = [step_of(5, 6), step_of(5, 7)]
    final += [(12, 2, 2 + u // 2, slot_of(3, 2 + u // 2, u % 2)) for u in range(4)]
    final += [last_step(u) for u in range(8)] + [None, None]
    for u in range(14):
        top, shrink = advance(u, final[u + 2], final[u + 1], final[u], top, shrink)
        if u >= 7 and u % 2:
            finish(3 - (u - 7) // 2)

    for n in (1, 2, 3):
        for c in ret_copies(n):
            c.wait_recv()

    for b in range(BRANCHES):
        lses = [own_m[b] + jnp.log(own_l[b]) * LOG2E, ret_lse[0, b : b + 1, :]]
        lses += [back_lse[n, b : b + 1, :] for n in (1, 2, 3)]
        peak = functools.reduce(jnp.maximum, lses)
        scales = [jnp.exp2(t - peak) for t in lses]
        denom = sum(scales)
        merged = own_acc[b] * (scales[0] / (denom * own_l[b]))
        outs = [ret[0, b]] + [back[n, b] for n in (1, 2, 3)]
        for a, o in zip(scales[1:], outs):
            merged = merged + o.astype(jnp.float32) * (a / denom)
        turned = jnp.transpose(merged).astype(jnp.bfloat16)
        for h in range(HEADS):
            attn[b * SLOTS : (b + 1) * SLOTS, h * HEAD : (h + 1) * HEAD] = turned[h * SLOTS : (h + 1) * SLOTS, :]
    copy_w.wait()

    width = w_buf.shape[1] // CHUNKS
    mid = width // 2
    share = part.shape[2]
    right, left, far = lax.rem(x + 1, 4), lax.rem(x + 3, 4), lax.rem(x + 2, 4)

    def pair_copy(n):
        return remote(pair_send.at[n], pair_recv.at[n], pair_ssem.at[n], pair_rsem.at[n], partner)

    def d_copies(n):
        return tuple(
            remote(d_send.at[n, i], d_recv.at[n, i], d_ssem.at[n, i], d_rsem.at[n, i], device)
            for i, device in ((0, x_right), (1, x_left))
        )

    def r_copy(n, i, half):
        return remote(
            r_send.at[n, i, half], r_recv.at[n, i, half], r_ssem.at[n, i, half], r_rsem.at[n, i, half],
            (x_right, x_left)[i],
        )

    def r_copies(n):
        return tuple(r_copy(n, i, half) for i in range(2) for half in range(2))

    def project(n):
        columns = pl.ds(pl.multiple_of(n * width, width), width)
        part[n] = dot(attn[...], w_buf[:, columns], NN).reshape(8, share, width)
        for i in range(4):
            pair_send[n, i] = part[n, 2 * i + 1 - core].astype(jnp.bfloat16)
        pair_copy(n).start()

    def pair_sum(n):
        pair_copy(n).wait_recv()
        for i in range(4):
            total[n, i] = part[n, 2 * i + core] + pair_recv[n, i].astype(jnp.float32)
        d_send[n, 0] = total[n, far, :, :mid].astype(jnp.bfloat16)
        d_send[n, 1] = total[n, far, :, mid:].astype(jnp.bfloat16)
        for c in d_copies(n):
            c.start()
        r_send[n, 0, 1] = total[n, right, :, mid:].astype(jnp.bfloat16)
        r_send[n, 1, 0] = total[n, left, :, :mid].astype(jnp.bfloat16)
        r_copy(n, 0, 1).start()
        r_copy(n, 1, 0).start()

    def ring_sum(n):
        for c in d_copies(n):
            c.wait_recv()
        r_send[n, 0, 0] = (total[n, right, :, :mid] + d_recv[n, 0].astype(jnp.float32)).astype(jnp.bfloat16)
        r_send[n, 1, 1] = (total[n, left, :, mid:] + d_recv[n, 1].astype(jnp.float32)).astype(jnp.bfloat16)
        r_copy(n, 0, 0).start()
        r_copy(n, 1, 1).start()

    def last_sum(n):
        for c in r_copies(n):
            c.wait_recv()
        for half in range(2):
            columns = pl.ds(pl.multiple_of(n * width + half * mid, mid), mid)
            out_ref[:, columns] = (
                total[n, x, :, half * mid : (half + 1) * mid]
                + r_recv[n, 0, half].astype(jnp.float32)
                + r_recv[n, 1, half].astype(jnp.float32)
            ).astype(jnp.bfloat16)

    def tail(i, carry):
        for lag, stage in zip(LAGS, (project, pair_sum, ring_sum, last_sum)):
            n = i - lag

            @pl.when((n >= 0) & (n < CHUNKS))
            def _():
                stage(n)

        return carry

    lax.fori_loop(0, CHUNKS + LAGS[-1], tail, 0)

    for c in sends:
        c.wait_send()
    for n in (1, 2, 3):
        for c in ret_copies(n):
            c.wait_send()

    def drain(n, carry):
        pair_copy(n).wait_send()
        for c in d_copies(n) + r_copies(n):
            c.wait_send()
        return carry

    lax.fori_loop(0, CHUNKS, drain, 0)


def body(queries, keys, values, own_keys, own_values, owners, lengths, out_weight):
    share = queries.shape[0] // 8
    depth, columns = out_weight.shape
    width = columns // CHUNKS
    mid = width // 2
    bf16, f32, i32 = jnp.bfloat16, jnp.float32, jnp.int32
    vmem = pltpu.VMEM
    dma = pltpu.SemaphoreType.DMA
    anywhere = pl.BlockSpec(memory_space=pl.ANY)
    inside = pl.BlockSpec(memory_space=pltpu.VMEM)
    scalars = pl.BlockSpec(memory_space=pltpu.SMEM)
    return pl.pallas_call(
        kernel,
        out_shape=jax.ShapeDtypeStruct((share, columns), bf16),
        in_specs=[anywhere, anywhere, anywhere, inside, inside, scalars, scalars, anywhere],
        out_specs=inside,
        scratch_shapes=[
            vmem((depth, columns), bf16),
            vmem((16, STRIP, HEAD), bf16),
            vmem((16, HEAD, STRIP), bf16),
            vmem((2 * HALF, HEAD), bf16),
            vmem((4, BRANCHES, SLOTS, HEADS * HEAD), bf16),
            vmem((4 * BRANCHES, COLS, 2 * HEAD), bf16),
            vmem((8, 128), i32),
            vmem((4, 8, 128), i32),
            pltpu.SMEM((8, 128), i32),
            pltpu.SMEM((32,), i32),
            pltpu.SMEM((64,), i32),
            vmem((HALF, COLS), f32),
            vmem((HALF, COLS), f32),
            vmem((HALF, COLS), bf16),
            vmem((HALF, COLS), bf16),
            vmem((32, 1, COLS), f32),
            vmem((32, 1, COLS), f32),
            vmem((32, HEAD, COLS), f32),
            vmem((BRANCHES, 1, COLS), f32),
            vmem((BRANCHES, 1, COLS), f32),
            vmem((BRANCHES, HEAD, COLS), f32),
            vmem((4, BRANCHES, HEAD, COLS), bf16),
            vmem((4, 8, COLS), f32),
            vmem((4, BRANCHES, HEAD, COLS), bf16),
            vmem((4, 8, COLS), f32),
            vmem((BRANCHES * SLOTS, depth), bf16),
            vmem((CHUNKS, 8, share, width), f32),
            vmem((CHUNKS, 4, share, width), f32),
            vmem((CHUNKS, 4, share, width), bf16),
            vmem((CHUNKS, 4, share, width), bf16),
            vmem((CHUNKS, 2, share, mid), bf16),
            vmem((CHUNKS, 2, share, mid), bf16),
            vmem((CHUNKS, 2, 2, share, mid), bf16),
            vmem((CHUNKS, 2, 2, share, mid), bf16),
            dma((4,)),
            dma((5,)), dma((5,)), dma((4,)), dma((4,)),
            dma((2, 16)), dma((2, 16)),
            dma((2, 4)), dma((2, 4)),
            dma((CHUNKS,)), dma((CHUNKS,)),
            dma((CHUNKS, 2)), dma((CHUNKS, 2)), dma((CHUNKS, 2, 2)), dma((CHUNKS, 2, 2)),
        ],
        compiler_params=pltpu.CompilerParams(
            collective_id=0, has_side_effects=True, vmem_limit_bytes=58 * 1024 * 1024
        ),
        name="branch_attention",
    )(
        queries.reshape(BRANCHES, SLOTS, queries.shape[1]),
        keys.reshape(4, STRIP, HEAD), values, own_keys, own_values, owners, lengths, out_weight,
    )


def solution(mesh):
    in_specs = (
        P("seq", "tp"),
        P("seq", "tp"),
        P("seq", "tp"),
        P("seq", "tp"),
        P("seq", "tp"),
        P("seq", None),
        P("seq"),
        P("tp", None),
    )
    out_specs = P(("seq", "tp"), None)
    return jax.shard_map(body, mesh=mesh, in_specs=in_specs, out_specs=out_specs, check_vma=False)
```

```python
import functools

import jax
import jax.numpy as jnp
from jax import lax
from jax.experimental import pallas as pl
from jax.experimental.pallas import tpu as pltpu
from jax.sharding import PartitionSpec as P

HEAD = 128
SLOTS = 32
BRANCHES = 4
FAN = 4
HEADS = 8
COLS = HEADS * SLOTS
HALF = 1024
STRIP = 512
CHUNKS = 4
LAGS = (0, 1, 3, 5)
LOG2E = 1.4426950408889634
SCALE = HEAD**-0.5 * LOG2E
LOW = -1e30
MESH = pl.DeviceIdType.MESH
NT = (((1,), (1,)), ((), ()))
NN = (((1,), (0,)), ((), ()))


def dot(a, b, dims):
    return lax.dot_general(a, b, dims, preferred_element_type=jnp.float32)


def await_bytes(ref, sem):
    pltpu.make_async_copy(ref, ref, sem).wait()


def kernel(
    q_hbm, k_hbm, v_hbm, ck_ref, cv_ref, owners_ref, lengths_ref, w_hbm,
    out_ref,
    w_buf, kp, vp, v_own, qbuf, qs, own_vec, own_buf, raw, tab, inv,
    s_a, s_b, p_a, p_b, m_ref, l_ref, acc, own_m, own_l, own_acc,
    ret, ret_lse, back, back_lse, attn,
    part, total, pair_send, pair_recv, d_send, d_recv, r_send, r_recv,
    loc_sem, q_ssem, q_rsem, o_ssem, o_rsem, kv_ssem, kv_rsem,
    ret_ssem, ret_rsem, pair_ssem, pair_rsem, d_ssem, d_rsem, r_ssem, r_rsem,
):
    seq = lax.axis_index("seq")
    tp = lax.axis_index("tp")
    y, z = lax.div(seq, 4), lax.rem(seq, 4)
    x, core = lax.div(tp, 2), lax.rem(tp, 2)
    kv_pos = (1 - core) * z + core * y
    q_pos = (1 - core) * y + core * z

    def kv_seq(step):
        a = lax.rem(kv_pos + step, 4)
        return (1 - core) * (q_pos * 4 + a) + core * (a * 4 + q_pos)

    def q_seq(step):
        a = lax.rem(q_pos + step, 4)
        return (1 - core) * (a * 4 + kv_pos) + core * (kv_pos * 4 + a)

    kv_right, kv_left = (kv_seq(1), tp), (kv_seq(3), tp)
    peers = {1: (q_seq(3), tp), 2: (q_seq(1), tp), 3: (q_seq(2), tp)}
    mirror = {1: 2, 2: 1, 3: 3}
    partner = (seq, x * 2 + 1 - core)
    x_right = (seq, lax.rem(x + 1, 4) * 2 + core)
    x_left = (seq, lax.rem(x + 3, 4) * 2 + core)
    everyone = (kv_right, kv_left, peers[1], peers[2], peers[3], partner, x_right, x_left)

    def remote(src, dst, ssem, rsem, device):
        return pltpu.make_async_remote_copy(
            src_ref=src, dst_ref=dst, send_sem=ssem, recv_sem=rsem, device_id=device, device_id_type=MESH
        )

    barrier = pltpu.get_barrier_semaphore()
    for device in everyone:
        pl.semaphore_signal(barrier, inc=1, device_id=device, device_id_type=MESH)

    copy_v = pltpu.make_async_copy(v_hbm, v_own, loc_sem.at[0])
    copy_v.start()
    copy_q = pltpu.make_async_copy(q_hbm, qbuf.at[0], q_rsem.at[0])
    copy_q.start()
    copy_k = pltpu.make_async_copy(k_hbm, kp.at[pl.ds(0, 4)], loc_sem.at[1])
    copy_k.start()

    rows = lax.broadcasted_iota(jnp.int32, (8, 128), 0)
    lanes = lax.broadcasted_iota(jnp.int32, (8, 128), 1)
    vec = jnp.zeros((8, 128), jnp.int32)
    for b in range(BRANCHES):
        for f in range(FAN):
            vec = jnp.where((rows == b) & (lanes == f), owners_ref[b, f], vec)
    own_vec[...] = vec
    copy_o = pltpu.make_async_copy(own_vec, own_buf.at[0], o_rsem.at[0])
    copy_o.start()

    copy_v.wait()
    for n in (0, 2, 1, 3):
        vp[n] = jnp.transpose(v_own[pl.ds(n * STRIP, STRIP), :].astype(jnp.float32)).astype(jnp.bfloat16)
    pl.semaphore_wait(barrier, len(everyone))

    sends = []
    for j in (3, 1, 2):
        sends.append(remote(own_vec, own_buf.at[mirror[j]], o_ssem.at[j], o_rsem.at[mirror[j]], peers[j]))
        sends[-1].start()
    for j in (1, 2):
        sends.append(remote(q_hbm, qbuf.at[mirror[j]], q_ssem.at[j], q_rsem.at[mirror[j]], peers[j]))
        sends[-1].start()
    q_relay = [
        remote(qbuf.at[1, pl.ds(0, 2)], qbuf.at[3, pl.ds(0, 2)], q_ssem.at[3], q_rsem.at[3], peers[2]),
        remote(qbuf.at[2, pl.ds(2, 2)], qbuf.at[3, pl.ds(2, 2)], q_ssem.at[4], q_rsem.at[4], peers[1]),
    ]

    def kv_send(src, dst, count, device, which):
        buf = (kp, vp)[which]
        source_ref = k_hbm if which == 0 and src < 4 else buf
        return remote(
            source_ref.at[pl.ds(src, count)], buf.at[pl.ds(dst, count)],
            kv_ssem.at[which, dst], kv_rsem.at[which, dst], device,
        )

    def kv_await(quarter, count):
        for which, buf in ((0, kp), (1, vp)):
            await_bytes(buf.at[pl.ds(quarter, count)], kv_rsem.at[which, quarter])

    opening = [
        [kv_send(i, 4 + i, 1, kv_right, which) for which in range(2)]
        + [kv_send(2 + i, 6 + i, 1, kv_left, which) for which in range(2)]
        for i in range(2)
    ]
    closing = [
        kv_send(src, dst, 2, device, which)
        for which in range(2) for src, dst, device in ((2, 8, kv_right), (0, 10, kv_left))
    ]
    relay = [
        [kv_send(4 + i, 12 + i, 1, kv_right, which) for which in range(2)]
        + [kv_send(6 + i, 14 + i, 1, kv_left, which) for which in range(2)]
        for i in range(2)
    ]
    sends += q_relay + opening[0] + opening[1] + closing + relay[0] + relay[1]

    copy_k.wait()
    copy_w = pltpu.make_async_copy(w_hbm, w_buf, loc_sem.at[2])
    copy_w.start()

    m_ref[...] = jnp.full(m_ref.shape, LOW, jnp.float32)
    l_ref[...] = jnp.zeros(l_ref.shape, jnp.float32)
    acc[...] = jnp.zeros(acc.shape, jnp.float32)

    def slot_of(o, j, k):
        return o * 8 + j * 2 + k

    def stage(ahead, s_out, middle, top, s_in, p_out, behind, shrink, p_in):
        best = gain = next_shrink = None
        if ahead is not None:
            quarter, gap, j, s0 = ahead
            q_now = qs[j * BRANCHES + tab[s0]]
        if middle is not None:
            mid_slot = middle[3]
            old = m_ref[mid_slot]
            new = jnp.maximum(old, jnp.max(top, axis=0, keepdims=True))
            next_shrink = jnp.exp2(old - new)
            m_ref[mid_slot] = new
        for c in range(2):
            span = pl.ds(c * STRIP, STRIP)
            if ahead is not None:
                k_now = kp[quarter + c * gap]
                scores = dot(jnp.concatenate([k_now, k_now], axis=1), q_now, NT)
            if behind is not None:
                values = jnp.concatenate([vp[behind[0] + c * behind[1]], jnp.ones((16, STRIP), jnp.bfloat16)], axis=0)
                term = dot(values, p_in[span, :], NN)
                gain = term if gain is None else gain + term
            if middle is not None:
                p_out[span, :] = jnp.exp2(s_in[span, :] - new).astype(jnp.bfloat16)
            if ahead is not None:
                s_out[span, :] = scores
                here = jnp.max(scores.reshape(STRIP // 64, 64, COLS), axis=0)
                best = here if best is None else jnp.maximum(best, here)
        if behind is not None:
            s2 = behind[3]
            l_ref[s2] = l_ref[s2] * shrink + gain[HEAD : HEAD + 1]
            acc[s2] = acc[s2] * shrink + gain[:HEAD]
        if best is not None:
            best = jnp.max(best.reshape(8, 8, COLS), axis=0)
        return best, next_shrink

    def own_step(j, u):
        return 2 * (u // 2), 1, j, slot_of(0, j, u % 2)

    def near_step(piece, u):
        return 4 + 2 * piece, 1, u // 2, slot_of(1 + lax.rem(piece, 2), u // 2, u % 2)

    def far_step(j, u):
        return 12 + u // 2, 2, j, slot_of(3, j, u % 2)

    scores_of, probs_of = (s_a, s_b), (p_a, p_b)

    def advance(u, ahead, middle, behind, top, shrink):
        return stage(
            ahead, scores_of[u % 2], middle, top, scores_of[(u + 1) % 2], probs_of[(u + 1) % 2],
            behind, shrink, probs_of[u % 2],
        )

    group = [seq, kv_seq(3), kv_seq(1), kv_seq(2)]

    def own_rows():
        row = lax.broadcasted_iota(jnp.int32, (BRANCHES * SLOTS, COLS), 0)
        slot = lax.rem(lax.broadcasted_iota(jnp.int32, (BRANCHES * SLOTS, COLS), 1), SLOTS)
        ck = ck_ref[...]
        ck2 = jnp.concatenate([ck, ck], axis=1)
        cv_t = jnp.transpose(cv_ref[...].astype(jnp.float32)).astype(jnp.bfloat16)
        for b in range(BRANCHES):
            key = row - b * SLOTS
            allowed = (key >= 0) & (key <= slot) & (key < lengths_ref[b])
            scores = jnp.where(allowed, dot(ck2, qs[b], NT), LOW)
            top = jnp.max(scores, axis=0, keepdims=True)
            prob = jnp.where(allowed, jnp.exp2(scores - top), 0.0)
            own_m[b] = top
            own_l[b] = jnp.sum(prob, axis=0, keepdims=True)
            own_acc[b] = dot(cv_t, prob.astype(jnp.bfloat16), NN)

    def pass_on(n):
        for quarter, base in ((4 + n, 0), (6 + n, 2)):
            kv_await(quarter, 1)
            for c in relay[n][base : base + 2]:
                c.start()

    def find_slots(j, carry):
        await_bytes(own_buf.at[j], o_rsem.at[j])
        copy = pltpu.make_async_copy(own_buf.at[j], raw, loc_sem.at[3])
        copy.start()
        copy.wait()
        for o in range(4):
            count, first, second = jnp.int32(0), jnp.int32(0), jnp.int32(0)
            for b in range(BRANCHES):
                hit = raw[b, 0] == group[o]
                for f in range(1, FAN):
                    hit = hit | (raw[b, f] == group[o])
                inv[(o * 4 + j) * BRANCHES + b] = jnp.where(hit & (count < 2), count, -1)
                first = jnp.where(hit & (count == 0), b, first)
                second = jnp.where(hit & (count == 1), b, second)
                count = count + hit.astype(jnp.int32)
            tab[slot_of(o, j, 0)] = first
            tab[slot_of(o, j, 1)] = second
        return carry

    def split_queries(j, carry):
        for b in range(BRANCHES):
            stacked = jnp.concatenate([qbuf[j, b, :, pl.ds(h * HEAD, HEAD)] for h in range(HEADS)], axis=0)
            exact = stacked.astype(jnp.float32) * SCALE
            high = exact.astype(jnp.bfloat16)
            qs[j * BRANCHES + b, :, :HEAD] = high
            qs[j * BRANCHES + b, :, HEAD:] = (exact - high.astype(jnp.float32)).astype(jnp.bfloat16)
        return carry

    def own_round(j, carry):
        top, shrink = carry

        @pl.when(j == 1)
        def _():
            for n in (1, 2):
                await_bytes(qbuf.at[n], q_rsem.at[n])
                q_relay[n - 1].start()
            for c in closing:
                c.start()

        @pl.when(j == 3)
        def _():
            pass_on(0)
            await_bytes(qbuf.at[3, pl.ds(0, 2)], q_rsem.at[3])
            await_bytes(qbuf.at[3, pl.ds(2, 2)], q_rsem.at[4])

        split_queries(j, 0)
        steps = [own_step(j - 1, 2), own_step(j - 1, 3)] + [own_step(j, u) for u in range(4)]
        for u in range(4):
            top, shrink = advance(u, steps[u + 2], steps[u + 1], steps[u], top, shrink)
        return top, shrink

    def near_round(piece, carry):
        top, shrink = carry
        start = 1 - lax.div(piece + 3, 4)
        before = piece - 1 + start

        for n, quarter in ((2, 8), (3, 10)):

            @pl.when(piece == n)
            def _():
                kv_await(quarter, 2)

        def earlier(u):
            near, own = near_step(before, u), own_step(3, u - 4)
            return tuple(start * b + (1 - start) * a for a, b in zip(near, own))

        steps = [earlier(6), earlier(7)] + [near_step(piece, u) for u in range(8)]
        for u in range(8):
            top, shrink = advance(u, steps[u + 2], steps[u + 1], steps[u], top, shrink)
        return top, shrink

    find_slots(0, 0)
    await_bytes(qbuf.at[0], q_rsem.at[0])
    split_queries(0, 0)
    opened = [own_step(0, u) for u in range(4)]
    top = shrink = None
    for u in range(4):
        top, shrink = advance(
            u, opened[u], opened[u - 1] if u >= 1 else None, opened[u - 2] if u >= 2 else None, top, shrink
        )
    for c in opening[0] + opening[1]:
        c.start()
    own_rows()
    lax.fori_loop(1, 4, find_slots, 0)
    carry = lax.fori_loop(1, 4, own_round, (top, shrink))
    pass_on(1)
    top, shrink = lax.fori_loop(0, 4, near_round, carry)

    def ret_copies(j):
        return (
            remote(ret.at[j], back.at[mirror[j]], ret_ssem.at[0, j], ret_rsem.at[0, mirror[j]], peers[j]),
            remote(ret_lse.at[j], back_lse.at[mirror[j]], ret_ssem.at[1, j], ret_rsem.at[1, mirror[j]], peers[j]),
        )

    def finish(j):
        for b in range(BRANCHES):
            slots, tops, sums, oks = [], [], [], []
            for o in range(4):
                place = inv[(o * 4 + j) * BRANCHES + b]
                ok = place >= 0
                s = slot_of(o, j, jnp.where(ok, place, 0))
                slots.append(s)
                oks.append(ok)
                tops.append(jnp.where(ok, m_ref[s], LOW))
                sums.append(l_ref[s])
            peak = functools.reduce(jnp.maximum, tops)
            scales = [jnp.where(ok, jnp.exp2(t - peak), 0.0) for ok, t in zip(oks, tops)]
            denom = sum(a * l for a, l in zip(scales, sums))
            any_ok = denom > 0.0
            safe = jnp.where(any_ok, denom, 1.0)
            merged = sum(acc[s] * (a / safe) for s, a in zip(slots, scales))
            ret[j, b] = merged.astype(jnp.bfloat16)
            ret_lse[j, b : b + 1, :] = jnp.where(any_ok, peak + jnp.log(safe) * LOG2E, LOW)
        if j:
            for c in ret_copies(j):
                c.start()

    final = [near_step(3, 6), near_step(3, 7)]
    final += [far_step(j, u) for j in (3, 2, 1, 0) for u in range(4)] + [None, None]
    for u in range(18):
        if u in (0, 2):
            kv_await(12 + u // 2, 1)
            kv_await(14 + u // 2, 1)
        top, shrink = advance(u, final[u + 2], final[u + 1], final[u], top, shrink)
        if u >= 5 and u % 4 == 1:
            finish(3 - (u - 5) // 4)

    for n in (1, 2, 3):
        for c in ret_copies(n):
            c.wait_recv()

    for b in range(BRANCHES):
        lses = [own_m[b] + jnp.log(own_l[b]) * LOG2E, ret_lse[0, b : b + 1, :]]
        lses += [back_lse[n, b : b + 1, :] for n in (1, 2, 3)]
        peak = functools.reduce(jnp.maximum, lses)
        scales = [jnp.exp2(t - peak) for t in lses]
        denom = sum(scales)
        merged = own_acc[b] * (scales[0] / (denom * own_l[b]))
        outs = [ret[0, b]] + [back[n, b] for n in (1, 2, 3)]
        for a, o in zip(scales[1:], outs):
            merged = merged + o.astype(jnp.float32) * (a / denom)
        turned = jnp.transpose(merged).astype(jnp.bfloat16)
        for h in range(HEADS):
            attn[b * SLOTS : (b + 1) * SLOTS, h * HEAD : (h + 1) * HEAD] = turned[h * SLOTS : (h + 1) * SLOTS, :]
    copy_w.wait()

    width = w_buf.shape[1] // CHUNKS
    mid = width // 2
    share = part.shape[2]
    right, left, far = lax.rem(x + 1, 4), lax.rem(x + 3, 4), lax.rem(x + 2, 4)

    def pair_copy(n):
        return remote(pair_send.at[n], pair_recv.at[n], pair_ssem.at[n], pair_rsem.at[n], partner)

    def d_copies(n):
        return tuple(
            remote(d_send.at[n, i], d_recv.at[n, i], d_ssem.at[n, i], d_rsem.at[n, i], device)
            for i, device in ((0, x_right), (1, x_left))
        )

    def r_copy(n, i, half):
        return remote(
            r_send.at[n, i, half], r_recv.at[n, i, half], r_ssem.at[n, i, half], r_rsem.at[n, i, half],
            (x_right, x_left)[i],
        )

    def r_copies(n):
        return tuple(r_copy(n, i, half) for i in range(2) for half in range(2))

    def project(n):
        columns = pl.ds(pl.multiple_of(n * width, width), width)
        part[n] = dot(attn[...], w_buf[:, columns], NN).reshape(8, share, width)
        for i in range(4):
            pair_send[n, i] = part[n, 2 * i + 1 - core].astype(jnp.bfloat16)
        pair_copy(n).start()

    def pair_sum(n):
        pair_copy(n).wait_recv()
        for i in range(4):
            total[n, i] = part[n, 2 * i + core] + pair_recv[n, i].astype(jnp.float32)
        d_send[n, 0] = total[n, far, :, :mid].astype(jnp.bfloat16)
        d_send[n, 1] = total[n, far, :, mid:].astype(jnp.bfloat16)
        for c in d_copies(n):
            c.start()
        r_send[n, 0, 1] = total[n, right, :, mid:].astype(jnp.bfloat16)
        r_send[n, 1, 0] = total[n, left, :, :mid].astype(jnp.bfloat16)
        r_copy(n, 0, 1).start()
        r_copy(n, 1, 0).start()

    def ring_sum(n):
        for c in d_copies(n):
            c.wait_recv()
        r_send[n, 0, 0] = (total[n, right, :, :mid] + d_recv[n, 0].astype(jnp.float32)).astype(jnp.bfloat16)
        r_send[n, 1, 1] = (total[n, left, :, mid:] + d_recv[n, 1].astype(jnp.float32)).astype(jnp.bfloat16)
        r_copy(n, 0, 0).start()
        r_copy(n, 1, 1).start()

    def last_sum(n):
        for c in r_copies(n):
            c.wait_recv()
        for half in range(2):
            columns = pl.ds(pl.multiple_of(n * width + half * mid, mid), mid)
            out_ref[:, columns] = (
                total[n, x, :, half * mid : (half + 1) * mid]
                + r_recv[n, 0, half].astype(jnp.float32)
                + r_recv[n, 1, half].astype(jnp.float32)
            ).astype(jnp.bfloat16)

    def tail(i, carry):
        for lag, stage in zip(LAGS, (project, pair_sum, ring_sum, last_sum)):
            n = i - lag

            @pl.when((n >= 0) & (n < CHUNKS))
            def _():
                stage(n)

        return carry

    lax.fori_loop(0, CHUNKS + LAGS[-1], tail, 0)

    for c in sends:
        c.wait_send()
    for n in (1, 2, 3):
        for c in ret_copies(n):
            c.wait_send()

    def drain(n, carry):
        pair_copy(n).wait_send()
        for c in d_copies(n) + r_copies(n):
            c.wait_send()
        return carry

    lax.fori_loop(0, CHUNKS, drain, 0)


def body(queries, keys, values, own_keys, own_values, owners, lengths, out_weight):
    share = queries.shape[0] // 8
    depth, columns = out_weight.shape
    width = columns // CHUNKS
    mid = width // 2
    bf16, f32, i32 = jnp.bfloat16, jnp.float32, jnp.int32
    vmem = pltpu.VMEM
    dma = pltpu.SemaphoreType.DMA
    anywhere = pl.BlockSpec(memory_space=pl.ANY)
    inside = pl.BlockSpec(memory_space=pltpu.VMEM)
    scalars = pl.BlockSpec(memory_space=pltpu.SMEM)
    return pl.pallas_call(
        kernel,
        out_shape=jax.ShapeDtypeStruct((share, columns), bf16),
        in_specs=[anywhere, anywhere, anywhere, inside, inside, scalars, scalars, anywhere],
        out_specs=inside,
        scratch_shapes=[
            vmem((depth, columns), bf16),
            vmem((16, STRIP, HEAD), bf16),
            vmem((16, HEAD, STRIP), bf16),
            vmem((2 * HALF, HEAD), bf16),
            vmem((4, BRANCHES, SLOTS, HEADS * HEAD), bf16),
            vmem((4 * BRANCHES, COLS, 2 * HEAD), bf16),
            vmem((8, 128), i32),
            vmem((4, 8, 128), i32),
            pltpu.SMEM((8, 128), i32),
            pltpu.SMEM((32,), i32),
            pltpu.SMEM((64,), i32),
            vmem((HALF, COLS), f32),
            vmem((HALF, COLS), f32),
            vmem((HALF, COLS), bf16),
            vmem((HALF, COLS), bf16),
            vmem((32, 1, COLS), f32),
            vmem((32, 1, COLS), f32),
            vmem((32, HEAD, COLS), f32),
            vmem((BRANCHES, 1, COLS), f32),
            vmem((BRANCHES, 1, COLS), f32),
            vmem((BRANCHES, HEAD, COLS), f32),
            vmem((4, BRANCHES, HEAD, COLS), bf16),
            vmem((4, 8, COLS), f32),
            vmem((4, BRANCHES, HEAD, COLS), bf16),
            vmem((4, 8, COLS), f32),
            vmem((BRANCHES * SLOTS, depth), bf16),
            vmem((CHUNKS, 8, share, width), f32),
            vmem((CHUNKS, 4, share, width), f32),
            vmem((CHUNKS, 4, share, width), bf16),
            vmem((CHUNKS, 4, share, width), bf16),
            vmem((CHUNKS, 2, share, mid), bf16),
            vmem((CHUNKS, 2, share, mid), bf16),
            vmem((CHUNKS, 2, 2, share, mid), bf16),
            vmem((CHUNKS, 2, 2, share, mid), bf16),
            dma((4,)),
            dma((5,)), dma((5,)), dma((4,)), dma((4,)),
            dma((2, 16)), dma((2, 16)),
            dma((2, 4)), dma((2, 4)),
            dma((CHUNKS,)), dma((CHUNKS,)),
            dma((CHUNKS, 2)), dma((CHUNKS, 2)), dma((CHUNKS, 2, 2)), dma((CHUNKS, 2, 2)),
        ],
        compiler_params=pltpu.CompilerParams(
            collective_id=0, has_side_effects=True, vmem_limit_bytes=58 * 1024 * 1024
        ),
        name="branch_attention",
    )(
        queries.reshape(BRANCHES, SLOTS, queries.shape[1]),
        keys.reshape(4, STRIP, HEAD), values, own_keys, own_values, owners, lengths, out_weight,
    )


def solution(mesh):
    in_specs = (
        P("seq", "tp"),
        P("seq", "tp"),
        P("seq", "tp"),
        P("seq", "tp"),
        P("seq", "tp"),
        P("seq", None),
        P("seq"),
        P("tp", None),
    )
    out_specs = P(("seq", "tp"), None)
    return jax.shard_map(body, mesh=mesh, in_specs=in_specs, out_specs=out_specs, check_vma=False)
```

```python
import functools

import jax
import jax.numpy as jnp
from jax import lax
from jax.experimental import pallas as pl
from jax.experimental.pallas import tpu as pltpu
from jax.sharding import PartitionSpec as P

HEAD = 128
SLOTS = 32
BRANCHES = 4
FAN = 4
HEADS = 8
COLS = HEADS * SLOTS
HALF = 1024
STRIP = 512
CHUNKS = 4
LAGS = (0, 1, 3, 5)
LOG2E = 1.4426950408889634
SCALE = HEAD**-0.5 * LOG2E
LOW = -1e30
MESH = pl.DeviceIdType.MESH
NT = (((1,), (1,)), ((), ()))
NN = (((1,), (0,)), ((), ()))


def dot(a, b, dims):
    return lax.dot_general(a, b, dims, preferred_element_type=jnp.float32)


def await_bytes(ref, sem):
    pltpu.make_async_copy(ref, ref, sem).wait()


def kernel(
    q_hbm, k_hbm, v_hbm, ck_ref, cv_ref, owners_ref, lengths_ref, w_hbm,
    out_ref,
    w_buf, kp, vp, v_own, qbuf, qs, own_vec, own_buf, raw, tab, inv,
    s_a, s_b, p_a, p_b, m_ref, l_ref, acc, own_m, own_l, own_acc,
    ret, ret_lse, back, back_lse, attn,
    part, total, pair_send, pair_recv, d_send, d_recv, r_send, r_recv,
    loc_sem, q_ssem, q_rsem, o_ssem, o_rsem, kv_ssem, kv_rsem,
    ret_ssem, ret_rsem, pair_ssem, pair_rsem, d_ssem, d_rsem, r_ssem, r_rsem,
):
    seq = lax.axis_index("seq")
    tp = lax.axis_index("tp")
    y, z = lax.div(seq, 4), lax.rem(seq, 4)
    x, core = lax.div(tp, 2), lax.rem(tp, 2)
    kv_pos = (1 - core) * z + core * y
    q_pos = (1 - core) * y + core * z

    def kv_seq(step):
        a = lax.rem(kv_pos + step, 4)
        return (1 - core) * (q_pos * 4 + a) + core * (a * 4 + q_pos)

    def q_seq(step):
        a = lax.rem(q_pos + step, 4)
        return (1 - core) * (a * 4 + kv_pos) + core * (kv_pos * 4 + a)

    kv_right, kv_left = (kv_seq(1), tp), (kv_seq(3), tp)
    peers = {1: (q_seq(3), tp), 2: (q_seq(1), tp), 3: (q_seq(2), tp)}
    mirror = {1: 2, 2: 1, 3: 3}
    partner = (seq, x * 2 + 1 - core)
    x_right = (seq, lax.rem(x + 1, 4) * 2 + core)
    x_left = (seq, lax.rem(x + 3, 4) * 2 + core)
    everyone = (kv_right, kv_left, peers[1], peers[2], peers[3], partner, x_right, x_left)

    def remote(src, dst, ssem, rsem, device):
        return pltpu.make_async_remote_copy(
            src_ref=src, dst_ref=dst, send_sem=ssem, recv_sem=rsem, device_id=device, device_id_type=MESH
        )

    barrier = pltpu.get_barrier_semaphore()
    for device in everyone:
        pl.semaphore_signal(barrier, inc=1, device_id=device, device_id_type=MESH)

    copy_v = pltpu.make_async_copy(v_hbm, v_own, loc_sem.at[0])
    copy_v.start()
    copy_q = pltpu.make_async_copy(q_hbm, qbuf.at[0], q_rsem.at[0])
    copy_q.start()
    copy_k = pltpu.make_async_copy(k_hbm, kp.at[pl.ds(0, 4)], loc_sem.at[1])
    copy_k.start()

    rows = lax.broadcasted_iota(jnp.int32, (8, 128), 0)
    lanes = lax.broadcasted_iota(jnp.int32, (8, 128), 1)
    vec = jnp.zeros((8, 128), jnp.int32)
    for b in range(BRANCHES):
        for f in range(FAN):
            vec = jnp.where((rows == b) & (lanes == f), owners_ref[b, f], vec)
    own_vec[...] = vec
    copy_o = pltpu.make_async_copy(own_vec, own_buf.at[0], o_rsem.at[0])
    copy_o.start()

    copy_v.wait()
    for n in (0, 2, 1, 3):
        vp[n] = jnp.transpose(v_own[pl.ds(n * STRIP, STRIP), :].astype(jnp.float32)).astype(jnp.bfloat16)
    m_ref[...] = jnp.full(m_ref.shape, LOW, jnp.float32)
    l_ref[...] = jnp.zeros(l_ref.shape, jnp.float32)
    acc[...] = jnp.zeros(acc.shape, jnp.float32)
    pl.semaphore_wait(barrier, len(everyone))

    sends = []
    for j in (3, 1, 2):
        sends.append(remote(own_vec, own_buf.at[mirror[j]], o_ssem.at[j], o_rsem.at[mirror[j]], peers[j]))
        sends[-1].start()
    for j in (1, 2):
        sends.append(remote(q_hbm, qbuf.at[mirror[j]], q_ssem.at[j], q_rsem.at[mirror[j]], peers[j]))
        sends[-1].start()
    q_relay = [
        remote(qbuf.at[1, pl.ds(0, 2)], qbuf.at[3, pl.ds(0, 2)], q_ssem.at[3], q_rsem.at[3], peers[2]),
        remote(qbuf.at[2, pl.ds(2, 2)], qbuf.at[3, pl.ds(2, 2)], q_ssem.at[4], q_rsem.at[4], peers[1]),
    ]

    def kv_send(src, dst, count, device, which):
        buf = (kp, vp)[which]
        source_ref = k_hbm if which == 0 and src < 4 else buf
        return remote(
            source_ref.at[pl.ds(src, count)], buf.at[pl.ds(dst, count)],
            kv_ssem.at[which, dst], kv_rsem.at[which, dst], device,
        )

    def kv_await(quarter, count):
        for which, buf in ((0, kp), (1, vp)):
            await_bytes(buf.at[pl.ds(quarter, count)], kv_rsem.at[which, quarter])

    opening = [
        [kv_send(i, 4 + i, 1, kv_right, which) for which in range(2)]
        + [kv_send(2 + i, 6 + i, 1, kv_left, which) for which in range(2)]
        for i in range(2)
    ]
    closing = [
        kv_send(src, dst, 2, device, which)
        for which in range(2) for src, dst, device in ((2, 8, kv_right), (0, 10, kv_left))
    ]
    relay = [
        [kv_send(4 + i, 12 + i, 1, kv_right, which) for which in range(2)]
        + [kv_send(6 + i, 14 + i, 1, kv_left, which) for which in range(2)]
        for i in range(2)
    ]
    sends += q_relay + opening[0] + opening[1] + closing + relay[0] + relay[1]

    copy_k.wait()
    copy_w = pltpu.make_async_copy(w_hbm, w_buf, loc_sem.at[2])
    copy_w.start()

    def slot_of(o, j, k):
        return o * 8 + j * 2 + k

    def stage(ahead, s_out, middle, top, s_in, p_out, behind, shrink, p_in):
        best = gain = next_shrink = None
        if ahead is not None:
            quarter, gap, j, s0 = ahead
            q_now = qs[j * BRANCHES + tab[s0]]
        if middle is not None:
            mid_slot = middle[3]
            old = m_ref[mid_slot]
            new = jnp.maximum(old, jnp.max(top, axis=0, keepdims=True))
            next_shrink = jnp.exp2(old - new)
            m_ref[mid_slot] = new
        for c in range(2):
            span = pl.ds(c * STRIP, STRIP)
            if ahead is not None:
                k_now = kp[quarter + c * gap]
                scores = dot(jnp.concatenate([k_now, k_now], axis=1), q_now, NT)
            if behind is not None:
                values = jnp.concatenate([vp[behind[0] + c * behind[1]], jnp.ones((16, STRIP), jnp.bfloat16)], axis=0)
                term = dot(values, p_in[span, :], NN)
                gain = term if gain is None else gain + term
            if middle is not None:
                p_out[span, :] = jnp.exp2(s_in[span, :] - new).astype(jnp.bfloat16)
            if ahead is not None:
                s_out[span, :] = scores
                here = jnp.max(scores.reshape(STRIP // 64, 64, COLS), axis=0)
                best = here if best is None else jnp.maximum(best, here)
        if behind is not None:
            s2 = behind[3]
            l_ref[s2] = l_ref[s2] * shrink + gain[HEAD : HEAD + 1]
            acc[s2] = acc[s2] * shrink + gain[:HEAD]
        if best is not None:
            best = jnp.max(best.reshape(8, 8, COLS), axis=0)
        return best, next_shrink

    def own_step(j, u):
        return 2 * (u // 2), 1, j, slot_of(0, j, u % 2)

    def near_step(piece, u):
        return 4 + 2 * piece, 1, u // 2, slot_of(1 + lax.rem(piece, 2), u // 2, u % 2)

    def far_step(j, u):
        return 12 + u // 2, 2, j, slot_of(3, j, u % 2)

    scores_of, probs_of = (s_a, s_b), (p_a, p_b)

    def advance(u, ahead, middle, behind, top, shrink):
        return stage(
            ahead, scores_of[u % 2], middle, top, scores_of[(u + 1) % 2], probs_of[(u + 1) % 2],
            behind, shrink, probs_of[u % 2],
        )

    group = [seq, kv_seq(3), kv_seq(1), kv_seq(2)]

    def own_rows():
        row = lax.broadcasted_iota(jnp.int32, (BRANCHES * SLOTS, COLS), 0)
        slot = lax.rem(lax.broadcasted_iota(jnp.int32, (BRANCHES * SLOTS, COLS), 1), SLOTS)
        ck = ck_ref[...]
        ck2 = jnp.concatenate([ck, ck], axis=1)
        cv_t = jnp.transpose(cv_ref[...].astype(jnp.float32)).astype(jnp.bfloat16)
        for b in range(BRANCHES):
            key = row - b * SLOTS
            allowed = (key >= 0) & (key <= slot) & (key < lengths_ref[b])
            scores = jnp.where(allowed, dot(ck2, qs[b], NT), LOW)
            top = jnp.max(scores, axis=0, keepdims=True)
            prob = jnp.where(allowed, jnp.exp2(scores - top), 0.0)
            own_m[b] = top
            own_l[b] = jnp.sum(prob, axis=0, keepdims=True)
            own_acc[b] = dot(cv_t, prob.astype(jnp.bfloat16), NN)

    def pass_on(n):
        for quarter, base in ((4 + n, 0), (6 + n, 2)):
            kv_await(quarter, 1)
            for c in relay[n][base : base + 2]:
                c.start()

    def find_slots(j, carry):
        await_bytes(own_buf.at[j], o_rsem.at[j])
        copy = pltpu.make_async_copy(own_buf.at[j], raw, loc_sem.at[3])
        copy.start()
        copy.wait()
        for o in range(4):
            count, first, second = jnp.int32(0), jnp.int32(0), jnp.int32(0)
            for b in range(BRANCHES):
                hit = raw[b, 0] == group[o]
                for f in range(1, FAN):
                    hit = hit | (raw[b, f] == group[o])
                inv[(o * 4 + j) * BRANCHES + b] = jnp.where(hit & (count < 2), count, -1)
                first = jnp.where(hit & (count == 0), b, first)
                second = jnp.where(hit & (count == 1), b, second)
                count = count + hit.astype(jnp.int32)
            tab[slot_of(o, j, 0)] = first
            tab[slot_of(o, j, 1)] = second
        return carry

    def split_queries(j, carry):
        for b in range(BRANCHES):
            stacked = jnp.concatenate([qbuf[j, b, :, pl.ds(h * HEAD, HEAD)] for h in range(HEADS)], axis=0)
            exact = stacked.astype(jnp.float32) * SCALE
            high = exact.astype(jnp.bfloat16)
            qs[j * BRANCHES + b, :, :HEAD] = high
            qs[j * BRANCHES + b, :, HEAD:] = (exact - high.astype(jnp.float32)).astype(jnp.bfloat16)
        return carry

    def own_round(j, carry):
        top, shrink = carry

        @pl.when(j == 1)
        def _():
            for n in (1, 2):
                await_bytes(qbuf.at[n], q_rsem.at[n])
                q_relay[n - 1].start()
            for c in closing:
                c.start()

        @pl.when(j == 3)
        def _():
            pass_on(0)
            await_bytes(qbuf.at[3, pl.ds(0, 2)], q_rsem.at[3])
            await_bytes(qbuf.at[3, pl.ds(2, 2)], q_rsem.at[4])

        split_queries(j, 0)
        steps = [own_step(j - 1, 2), own_step(j - 1, 3)] + [own_step(j, u) for u in range(4)]
        for u in range(4):
            top, shrink = advance(u, steps[u + 2], steps[u + 1], steps[u], top, shrink)
        return top, shrink

    def near_round(piece, carry):
        top, shrink = carry
        start = 1 - lax.div(piece + 3, 4)
        before = piece - 1 + start

        for n, quarter in ((2, 8), (3, 10)):

            @pl.when(piece == n)
            def _():
                kv_await(quarter, 2)

        def earlier(u):
            near, own = near_step(before, u), own_step(3, u - 4)
            return tuple(start * b + (1 - start) * a for a, b in zip(near, own))

        steps = [earlier(6), earlier(7)] + [near_step(piece, u) for u in range(8)]
        for u in range(8):
            top, shrink = advance(u, steps[u + 2], steps[u + 1], steps[u], top, shrink)
        return top, shrink

    find_slots(0, 0)
    await_bytes(qbuf.at[0], q_rsem.at[0])
    split_queries(0, 0)
    opened = [own_step(0, u) for u in range(4)]
    top = shrink = None
    for u in range(4):
        top, shrink = advance(
            u, opened[u], opened[u - 1] if u >= 1 else None, opened[u - 2] if u >= 2 else None, top, shrink
        )
    for c in opening[0] + opening[1]:
        c.start()
    own_rows()
    lax.fori_loop(1, 4, find_slots, 0)
    carry = lax.fori_loop(1, 4, own_round, (top, shrink))
    pass_on(1)
    top, shrink = lax.fori_loop(0, 4, near_round, carry)

    def ret_copies(j):
        return (
            remote(ret.at[j], back.at[mirror[j]], ret_ssem.at[0, j], ret_rsem.at[0, mirror[j]], peers[j]),
            remote(ret_lse.at[j], back_lse.at[mirror[j]], ret_ssem.at[1, j], ret_rsem.at[1, mirror[j]], peers[j]),
        )

    def finish(j):
        for b in range(BRANCHES):
            slots, tops, sums, oks = [], [], [], []
            for o in range(4):
                place = inv[(o * 4 + j) * BRANCHES + b]
                ok = place >= 0
                s = slot_of(o, j, jnp.where(ok, place, 0))
                slots.append(s)
                oks.append(ok)
                tops.append(jnp.where(ok, m_ref[s], LOW))
                sums.append(l_ref[s])
            peak = functools.reduce(jnp.maximum, tops)
            scales = [jnp.where(ok, jnp.exp2(t - peak), 0.0) for ok, t in zip(oks, tops)]
            denom = sum(a * l for a, l in zip(scales, sums))
            any_ok = denom > 0.0
            safe = jnp.where(any_ok, denom, 1.0)
            merged = sum(acc[s] * (a / safe) for s, a in zip(slots, scales))
            ret[j, b] = merged.astype(jnp.bfloat16)
            ret_lse[j, b : b + 1, :] = jnp.where(any_ok, peak + jnp.log(safe) * LOG2E, LOW)
        if j:
            for c in ret_copies(j):
                c.start()

    final = [near_step(3, 6), near_step(3, 7)]
    final += [far_step(j, u) for j in (3, 2, 1, 0) for u in range(4)] + [None, None]
    for u in range(18):
        if u in (0, 2):
            kv_await(12 + u // 2, 1)
            kv_await(14 + u // 2, 1)
        top, shrink = advance(u, final[u + 2], final[u + 1], final[u], top, shrink)
        if u >= 5 and u % 4 == 1:
            finish(3 - (u - 5) // 4)

    for n in (1, 2, 3):
        for c in ret_copies(n):
            c.wait_recv()

    for b in range(BRANCHES):
        lses = [own_m[b] + jnp.log(own_l[b]) * LOG2E, ret_lse[0, b : b + 1, :]]
        lses += [back_lse[n, b : b + 1, :] for n in (1, 2, 3)]
        peak = functools.reduce(jnp.maximum, lses)
        scales = [jnp.exp2(t - peak) for t in lses]
        denom = sum(scales)
        merged = own_acc[b] * (scales[0] / (denom * own_l[b]))
        outs = [ret[0, b]] + [back[n, b] for n in (1, 2, 3)]
        for a, o in zip(scales[1:], outs):
            merged = merged + o.astype(jnp.float32) * (a / denom)
        turned = jnp.transpose(merged).astype(jnp.bfloat16)
        for h in range(HEADS):
            attn[b * SLOTS : (b + 1) * SLOTS, h * HEAD : (h + 1) * HEAD] = turned[h * SLOTS : (h + 1) * SLOTS, :]
    copy_w.wait()

    width = w_buf.shape[1] // CHUNKS
    mid = width // 2
    share = part.shape[2]
    right, left, far = lax.rem(x + 1, 4), lax.rem(x + 3, 4), lax.rem(x + 2, 4)

    def pair_copy(n):
        return remote(pair_send.at[n], pair_recv.at[n], pair_ssem.at[n], pair_rsem.at[n], partner)

    def d_copies(n):
        return tuple(
            remote(d_send.at[n, i], d_recv.at[n, i], d_ssem.at[n, i], d_rsem.at[n, i], device)
            for i, device in ((0, x_right), (1, x_left))
        )

    def r_copy(n, i, half):
        return remote(
            r_send.at[n, i, half], r_recv.at[n, i, half], r_ssem.at[n, i, half], r_rsem.at[n, i, half],
            (x_right, x_left)[i],
        )

    def r_copies(n):
        return tuple(r_copy(n, i, half) for i in range(2) for half in range(2))

    def project(n):
        columns = pl.ds(pl.multiple_of(n * width, width), width)
        part[n] = dot(attn[...], w_buf[:, columns], NN).reshape(8, share, width)
        for i in range(4):
            pair_send[n, i] = part[n, 2 * i + 1 - core].astype(jnp.bfloat16)
        pair_copy(n).start()

    def pair_sum(n):
        pair_copy(n).wait_recv()
        for i in range(4):
            total[n, i] = part[n, 2 * i + core] + pair_recv[n, i].astype(jnp.float32)
        d_send[n, 0] = total[n, far, :, :mid].astype(jnp.bfloat16)
        d_send[n, 1] = total[n, far, :, mid:].astype(jnp.bfloat16)
        for c in d_copies(n):
            c.start()
        r_send[n, 0, 1] = total[n, right, :, mid:].astype(jnp.bfloat16)
        r_send[n, 1, 0] = total[n, left, :, :mid].astype(jnp.bfloat16)
        r_copy(n, 0, 1).start()
        r_copy(n, 1, 0).start()

    def ring_sum(n):
        for c in d_copies(n):
            c.wait_recv()
        r_send[n, 0, 0] = (total[n, right, :, :mid] + d_recv[n, 0].astype(jnp.float32)).astype(jnp.bfloat16)
        r_send[n, 1, 1] = (total[n, left, :, mid:] + d_recv[n, 1].astype(jnp.float32)).astype(jnp.bfloat16)
        r_copy(n, 0, 0).start()
        r_copy(n, 1, 1).start()

    def last_sum(n):
        for c in r_copies(n):
            c.wait_recv()
        for half in range(2):
            columns = pl.ds(pl.multiple_of(n * width + half * mid, mid), mid)
            out_ref[:, columns] = (
                total[n, x, :, half * mid : (half + 1) * mid]
                + r_recv[n, 0, half].astype(jnp.float32)
                + r_recv[n, 1, half].astype(jnp.float32)
            ).astype(jnp.bfloat16)

    def tail(i, carry):
        for lag, stage in zip(LAGS, (project, pair_sum, ring_sum, last_sum)):
            n = i - lag

            @pl.when((n >= 0) & (n < CHUNKS))
            def _():
                stage(n)

        return carry

    lax.fori_loop(0, CHUNKS + LAGS[-1], tail, 0)

    for c in sends:
        c.wait_send()
    for n in (1, 2, 3):
        for c in ret_copies(n):
            c.wait_send()

    def drain(n, carry):
        pair_copy(n).wait_send()
        for c in d_copies(n) + r_copies(n):
            c.wait_send()
        return carry

    lax.fori_loop(0, CHUNKS, drain, 0)


def body(queries, keys, values, own_keys, own_values, owners, lengths, out_weight):
    share = queries.shape[0] // 8
    depth, columns = out_weight.shape
    width = columns // CHUNKS
    mid = width // 2
    bf16, f32, i32 = jnp.bfloat16, jnp.float32, jnp.int32
    vmem = pltpu.VMEM
    dma = pltpu.SemaphoreType.DMA
    anywhere = pl.BlockSpec(memory_space=pl.ANY)
    inside = pl.BlockSpec(memory_space=pltpu.VMEM)
    scalars = pl.BlockSpec(memory_space=pltpu.SMEM)
    return pl.pallas_call(
        kernel,
        out_shape=jax.ShapeDtypeStruct((share, columns), bf16),
        in_specs=[anywhere, anywhere, anywhere, inside, inside, scalars, scalars, anywhere],
        out_specs=inside,
        scratch_shapes=[
            vmem((depth, columns), bf16),
            vmem((16, STRIP, HEAD), bf16),
            vmem((16, HEAD, STRIP), bf16),
            vmem((2 * HALF, HEAD), bf16),
            vmem((4, BRANCHES, SLOTS, HEADS * HEAD), bf16),
            vmem((4 * BRANCHES, COLS, 2 * HEAD), bf16),
            vmem((8, 128), i32),
            vmem((4, 8, 128), i32),
            pltpu.SMEM((8, 128), i32),
            pltpu.SMEM((32,), i32),
            pltpu.SMEM((64,), i32),
            vmem((HALF, COLS), f32),
            vmem((HALF, COLS), f32),
            vmem((HALF, COLS), bf16),
            vmem((HALF, COLS), bf16),
            vmem((32, 1, COLS), f32),
            vmem((32, 1, COLS), f32),
            vmem((32, HEAD, COLS), f32),
            vmem((BRANCHES, 1, COLS), f32),
            vmem((BRANCHES, 1, COLS), f32),
            vmem((BRANCHES, HEAD, COLS), f32),
            vmem((4, BRANCHES, HEAD, COLS), bf16),
            vmem((4, 8, COLS), f32),
            vmem((4, BRANCHES, HEAD, COLS), bf16),
            vmem((4, 8, COLS), f32),
            vmem((BRANCHES * SLOTS, depth), bf16),
            vmem((CHUNKS, 8, share, width), f32),
            vmem((CHUNKS, 4, share, width), f32),
            vmem((CHUNKS, 4, share, width), bf16),
            vmem((CHUNKS, 4, share, width), bf16),
            vmem((CHUNKS, 2, share, mid), bf16),
            vmem((CHUNKS, 2, share, mid), bf16),
            vmem((CHUNKS, 2, 2, share, mid), bf16),
            vmem((CHUNKS, 2, 2, share, mid), bf16),
            dma((4,)),
            dma((5,)), dma((5,)), dma((4,)), dma((4,)),
            dma((2, 16)), dma((2, 16)),
            dma((2, 4)), dma((2, 4)),
            dma((CHUNKS,)), dma((CHUNKS,)),
            dma((CHUNKS, 2)), dma((CHUNKS, 2)), dma((CHUNKS, 2, 2)), dma((CHUNKS, 2, 2)),
        ],
        compiler_params=pltpu.CompilerParams(
            collective_id=0, has_side_effects=True, vmem_limit_bytes=58 * 1024 * 1024
        ),
        name="branch_attention",
    )(
        queries.reshape(BRANCHES, SLOTS, queries.shape[1]),
        keys.reshape(4, STRIP, HEAD), values, own_keys, own_values, owners, lengths, out_weight,
    )


def solution(mesh):
    in_specs = (
        P("seq", "tp"),
        P("seq", "tp"),
        P("seq", "tp"),
        P("seq", "tp"),
        P("seq", "tp"),
        P("seq", None),
        P("seq"),
        P("tp", None),
    )
    out_specs = P(("seq", "tp"), None)
    return jax.shard_map(body, mesh=mesh, in_specs=in_specs, out_specs=out_specs, check_vma=False)
```
